256 devices in a mesh: section: 2 (over core), dp: 16 (over y, x), mp: 8 (over z).
Axes of the slice: x: 4, y: 4, z: 8, core: 2. Of those that a mesh axis runs over, the one named last changes fastest.
Arguments:
- mel_frames: bfloat16 [24576, 128], P('dp'), may hold values from -6 to 6
- utt_rows: int32 [64], replicated, may hold values from 48 to 96, as said below
- utt_owner: int32 [64], replicated, may hold values from 0 to 15, as said below
- utt_offset: int32 [64], replicated, may hold values from 0 to 12287, as said below
- conv1_w: bfloat16 [384, 1280], P(None, ('section', 'mp')), may hold values from -0.3125 to 0.3125
- conv2_w: bfloat16 [3840, 1280], P(None, ('section', 'mp')), may hold values from -0.09375 to 0.09375
- adapter_w: bfloat16 [2560, 4096], P(None, ('section', 'mp')), may hold values from -0.125 to 0.125
- text_rows: bfloat16 [12288, 4096], P('dp', ('section', 'mp')), may hold values from -6 to 6
- norm_gain: float32 [4096], replicated, may hold values from 0.5 to 1.5
- gate_w: bfloat16 [4096, 11008], P('dp', ('section', 'mp')), may hold values from -0.09375 to 0.09375
- up_w: bfloat16 [4096, 11008], P('dp', ('section', 'mp')), may hold values from -0.09375 to 0.09375
Outputs:
- hidden: bfloat16 [12288, 11008], P('dp', ('section', 'mp'))
The draws below stay inside these ranges and needn't reach their ends.
Inputs may be any that keep to these rules, and one draw needn't show every extreme that they name: `utt_rows`: the utterances of one dp index hold at most 384 rows together, and some index holds exactly that many. `utt_owner`: every dp index owns exactly 4 utterances. The utterances of one owner whose packed rows lie in one dp block of 768 rows hold at most 96 rows together, and some owner and block reach exactly 96. `utt_offset`: utterance u lies wholly within rows u * (192) to (u + 1) * 192 - 1.
All inputs are finite; a program needn't handle non-finite values.
Results may differ from the reference program's by a relative error of at most 0.0073.
Values may be sent and summed in bfloat16 or wider, within the bound.
No kernel may reach another device: no remote copies, remote signals or barrier semaphores. Data moves between devices by JAX's collectives and lax.ppermute only.
A program may use at most 64 MiB of HBM per device.

```python
import jax
import jax.numpy as jnp
from jax import lax

MELS = 128
C = 1280
D = 4096
FF = 11008
MAXROWS = 96
GAPMAX = 96
UTT_DEV = 4
P_DEV = 384
L_DEV = 768
UTTS = 64
LLM_ROWS = 12288
FRAMES = 24576
N_DP = 16


def draw_plan(key):
    key_order, key_rows, key_heavy, key_gaps = jax.random.split(key, 4)
    ordering = jax.random.permutation(key_order, N_DP).astype(jnp.int32)
    index_all = jnp.arange(UTTS, dtype=jnp.int32)
    block_index = index_all // UTT_DEV
    within = index_all % UTT_DEV
    owners = jnp.take(ordering, (block_index + within) % N_DP).astype(jnp.int32)
    lengths = jax.random.randint(key_rows, (UTTS,), MAXROWS // 2, MAXROWS + 1)
    heavy = jax.random.randint(key_heavy, (), 0, N_DP)
    lengths = jnp.where(owners == heavy, MAXROWS, lengths).astype(jnp.int32)
    region = MAXROWS + GAPMAX
    slack = jax.random.randint(key_gaps, (UTTS,), 0, 1 << 20) % (region - lengths + 1)
    offsets = (index_all * region + slack).astype(jnp.int32)
    return (lengths, owners, offsets)


def draw_utt_rows(key, part):
    return draw_plan(key)[0]


def draw_utt_owner(key, part):
    return draw_plan(key)[1]


def draw_utt_offset(key, part):
    return draw_plan(key)[2]


def shard_levels(own_key, shape, cuts, smallest, largest):
    def one(dim, parts):
        heights = jax.random.uniform(jax.random.fold_in(jax.random.fold_in(own_key, 6), dim), (parts,), jnp.float32, smallest / len(cuts), largest / len(cuts))
        return jnp.repeat(jnp.exp(heights), shape[dim] // parts).reshape((-1,) + (1,) * (len(shape) - dim - 1))

    factor_of = one(*cuts[0])
    for cut in cuts[1:]:
        factor_of = factor_of * one(*cut)
    return factor_of


def noise(own_key, extent, scale, limit, shards=(), kind=jnp.bfloat16):
    entries = jax.random.normal(own_key, extent, jnp.float32) * scale
    if len(shards) > 0:
        entries = shard_levels(own_key, extent, shards, -0.22, 0.18) * entries
    return jnp.clip(entries, min=-limit, max=limit).astype(kind)


def setup_inputs(seed: int = 0) -> dict:
    splits = jax.random.split(jax.random.key(seed), 12)
    return {
        "mel_frames": noise(splits[0], (FRAMES, MELS), 1.0, 6.0, ((0, 16),)),
        "utt_rows": draw_utt_rows(jax.random.fold_in(splits[11], 71), 0),
        "utt_owner": draw_utt_owner(jax.random.fold_in(splits[11], 71), 0),
        "utt_offset": draw_utt_offset(jax.random.fold_in(splits[11], 71), 0),
        "conv1_w": noise(splits[4], (3 * MELS, C), (3 * MELS) ** -0.5, 0.3125, ((1, 16),)),
        "conv2_w": noise(splits[5], (3 * C, C), (3 * C) ** -0.5, 0.09375, ((1, 16),)),
        "adapter_w": noise(splits[6], (2 * C, D), (2 * C) ** -0.5, 0.125, ((1, 16),)),
        "text_rows": noise(splits[7], (LLM_ROWS, D), 1.0, 6.0, ((0, 16), (1, 16))),
        "norm_gain": jnp.clip(1.0 + 0.1 * jax.random.normal(splits[8], (D,), jnp.float32), 0.5, 1.5),
        "gate_w": noise(splits[9], (D, FF), D ** -0.5, 0.09375, ((0, 16), (1, 16))),
        "up_w": noise(splits[10], (D, FF), D ** -0.5, 0.09375, ((0, 16), (1, 16))),
    }


def utterance_starts(utt_rows, utt_owner):
    order_index = jnp.arange(utt_rows.shape[0], dtype=jnp.int32)
    earlier = (utt_owner[None, :] == utt_owner[:, None]) & (order_index[None, :] < order_index[:, None])
    return lax.optimization_barrier(jnp.sum(jnp.where(earlier, utt_rows[None, :], 0), axis=1)).astype(jnp.int32)

def row_utterance(positions, first_row, lengths):
    inside = (positions[:, None] >= first_row[None, :]) & (positions[:, None] < (first_row + lengths)[None, :])
    order_index = jnp.arange(first_row.shape[0], dtype=jnp.int32)
    return (lax.optimization_barrier(jnp.sum(jnp.where(inside, order_index[None, :] + 1, 0), axis=1)) - 1).astype(jnp.int32)

def lookup(values_table, chosen):
    order_index = jnp.arange(values_table.shape[0], dtype=jnp.int32)
    return lax.optimization_barrier(jnp.sum(jnp.where(chosen[:, None] == order_index[None, :], values_table[None, :], 0), axis=1)).astype(jnp.int32)

def strided_conv(frames, segments, weight, stride):
    zero_row = jnp.zeros_like(frames[:1])
    no_segment = jnp.full((1,), -1, jnp.int32)
    before = jnp.concatenate([zero_row, frames[:-1]], 0)
    following = jnp.concatenate([frames[1:], zero_row], 0)
    seg_before = jnp.concatenate([no_segment, segments[:-1]], 0)
    seg_following = jnp.concatenate([segments[1:], no_segment], 0)
    before = jnp.where((seg_before == segments)[:, None], before, 0)
    following = jnp.where((seg_following == segments)[:, None], following, 0)
    stacked = jnp.concatenate([before[::stride], frames[::stride], following[::stride]], 1)
    output = jnp.dot(stacked, weight, preferred_element_type=jnp.float32)
    active = (segments[::stride] >= 0)[:, None]
    return jnp.where(active, jax.nn.gelu(output, approximate=False), 0.0).astype(jnp.bfloat16)

def normalize(rows_in, norm_gain):
    values = rows_in.astype(jnp.float32)
    mean_sq = lax.optimization_barrier(jnp.mean(values * values, axis=1, keepdims=True))
    return (values * lax.rsqrt(mean_sq + 1e-05) * norm_gain).astype(jnp.bfloat16)

def reference(mel_frames, utt_rows, utt_owner, utt_offset, conv1_w, conv2_w, adapter_w, text_rows, norm_gain, gate_w, up_w):
    starts = utterance_starts(utt_rows, utt_owner)
    first_row = utt_owner * P_DEV + starts
    pooled = jnp.arange(N_DP * P_DEV, dtype=jnp.int32)
    row_seg = row_utterance(pooled, first_row, utt_rows)
    frame_seg = jnp.repeat(row_seg, 4)
    first_maps = strided_conv(mel_frames, frame_seg, conv1_w, 1)
    second_maps = strided_conv(first_maps, frame_seg, conv2_w, 2)
    frame_pairs = second_maps.reshape(N_DP * P_DEV, 2 * C)
    speech = jnp.dot(frame_pairs, adapter_w, preferred_element_type=jnp.float32).astype(jnp.bfloat16)
    llm_pos = jnp.arange(N_DP * L_DEV, dtype=jnp.int32)
    llm_seg = row_utterance(llm_pos, utt_offset, utt_rows)
    source = jnp.where(llm_seg >= 0, lookup(first_row - utt_offset, llm_seg) + llm_pos, 0).astype(jnp.int32)
    picked = jnp.take(speech, source, axis=0)
    llm_in = jnp.where((llm_seg >= 0)[:, None], picked, text_rows)
    normed = normalize(llm_in, norm_gain)
    gate_sum = jnp.dot(normed, gate_w, preferred_element_type=jnp.float32)
    up_sum = jnp.dot(normed, up_w, preferred_element_type=jnp.float32)
    return (jax.nn.silu(gate_sum) * up_sum).astype(jnp.bfloat16)
```

```python
import functools

import jax
import jax.numpy as jnp
from jax import lax
from jax.experimental import pallas as pl
from jax.experimental.pallas import tpu as pltpu
from jax.sharding import PartitionSpec as P

MELS = 128
C = 1280
D = 4096
N_DP = 16
MAXROWS = 96
P_DEV = 384
L_DEV = 768
REGION = 192
CPART = 80
FPART = 688
KPART = 256
BF = jnp.bfloat16
F32 = jnp.float32
RING = (0, -1, 1, 2)


def grid_perm(dy, dx):
    return [
        (y * 4 + x, ((y + dy) % 4) * 4 + (x + dx) % 4) for y in range(4) for x in range(4)
    ]


def shift_x(a, step):
    return lax.ppermute(a, "dp", grid_perm(0, step))


def shift_y(a, step):
    return lax.ppermute(a, "dp", grid_perm(step, 0))


def shift_z(a, step):
    return lax.ppermute(a, "mp", [(i, (i + step) % 8) for i in range(8)])


def swap(a):
    return lax.ppermute(a, "section", [(0, 1), (1, 0)])


def ring4(a, shift):
    half = a.shape[0] // 2
    before = shift(a, 1)
    after = shift(a, -1)
    return a, before, after, shift(before[:half], 1), shift(after[half:], -1)


def ring_z(a):
    half = a.shape[0] // 2
    found = {0: a}
    up, down = a, a
    for hop in range(1, 4):
        up, down = shift_z(up, 1), shift_z(down, -1)
        found[8 - hop], found[hop] = up, down
    found[4] = jnp.concatenate([shift_z(up[:half], 1), shift_z(down[half:], -1)], 0)
    return [found[i] for i in range(8)]


def direct_z(a):
    return [a] + [shift_z(a, -k) for k in range(1, 8)]


def gelu(v):
    return 0.5 * v * (1.0 + lax.erf(v * (0.5**0.5)))


def vmem():
    return pl.BlockSpec(memory_space=pltpu.VMEM)


def smem():
    return pl.BlockSpec(memory_space=pltpu.SMEM)


def hbm():
    return pl.BlockSpec(memory_space=pl.ANY)


def encoder_kernel(info, x_ref, w1a_ref, w1b_ref, w2_ref, out_ref, w1, y):
    z, s = info[0], info[1]
    for d in range(8):
        peer = lax.rem(z + d, 8)
        for part, ref in ((s, w1a_ref), (1 - s, w1b_ref)):
            rows = pl.multiple_of((part * 8 + peer) * CPART, 16)
            w1[pl.ds(rows, CPART), :] = ref[d]
    x = x_ref[...]
    rows = 2 * MAXROWS
    row = lax.broadcasted_iota(jnp.int32, (rows, 1), 0)
    second = row >= MAXROWS
    first_of_slot = (row == 0) | (row == MAXROWS)
    last_of_slot = (row == MAXROWS - 1) | (row == rows - 1)
    length = jnp.where(second, info[3], info[2])
    active = (row - jnp.where(second, MAXROWS, 0)) < length
    head = x[:, :MELS].astype(F32)
    tail = x[:, 3 * MELS :].astype(F32)
    before = jnp.where(first_of_slot, 0.0, pltpu.roll(tail, 1, 0)).astype(BF)
    following = jnp.where(last_of_slot, 0.0, pltpu.roll(head, rows - 1, 0)).astype(BF)
    wide = jnp.concatenate([before, x, following], 1)
    for tile in range(C // 256):
        weight = w1[tile * 256 : (tile + 1) * 256, :]
        for q in range(4):
            total = lax.dot_general(
                wide[:, q * MELS : (q + 3) * MELS],
                weight,
                (((1,), (1,)), ((), ())),
                preferred_element_type=F32,
            )
            y[q, :, tile * 256 : (tile + 1) * 256] = jnp.where(active, gelu(total), 0.0).astype(BF)
    last = y[3].astype(F32)
    y_before = jnp.where(first_of_slot, 0.0, pltpu.roll(last, 1, 0)).astype(BF)
    dot = functools.partial(jnp.dot, preferred_element_type=F32)
    w_before, w_mid, w_after = w2_ref[:C], w2_ref[C : 2 * C], w2_ref[2 * C :]
    even = dot(y_before, w_before) + dot(y[0], w_mid) + dot(y[1], w_after)
    odd = dot(y[1], w_before) + dot(y[2], w_mid) + dot(y[3], w_after)
    both = jnp.concatenate([even, odd], 1)
    out_ref[...] = jnp.where(active, gelu(both), 0.0).astype(BF)


def encoder(info, x, w1a, w1b, w2):
    return pl.pallas_call(
        encoder_kernel,
        out_shape=jax.ShapeDtypeStruct((2 * MAXROWS, 4 * CPART), BF),
        in_specs=[smem(), vmem(), vmem(), vmem(), vmem()],
        out_specs=vmem(),
        scratch_shapes=[
            pltpu.VMEM((C, 3 * MELS), BF),
            pltpu.VMEM((4, 2 * MAXROWS, C), BF),
        ],
        compiler_params=pltpu.CompilerParams(vmem_limit_bytes=24 * 1024 * 1024),
        cost_estimate=pl.CostEstimate(
            flops=2 * 192 * 4 * (384 * C + 3840 * 80), bytes_accessed=5_000_000, transcendentals=0
        ),
        name="encoder",
    )(info, x, w1a, w1b, w2)


def adapter_kernel(info, *refs):
    pieces, w_ref, out_ref = refs[:8], refs[8], refs[9]
    z = info[0]
    total = jnp.dot(pieces[0][...], w_ref[z], preferred_element_type=F32)
    for d in range(1, 8):
        total += jnp.dot(pieces[d][...], w_ref[lax.rem(z + d, 8)], preferred_element_type=F32)
    out_ref[...] = total.astype(BF)


def adapter(info, pieces, w):
    return pl.pallas_call(
        adapter_kernel,
        out_shape=jax.ShapeDtypeStruct((2 * MAXROWS, 2 * KPART), BF),
        in_specs=[smem()] + [vmem()] * 9,
        out_specs=vmem(),
        compiler_params=pltpu.CompilerParams(vmem_limit_bytes=24 * 1024 * 1024),
        cost_estimate=pl.CostEstimate(
            flops=2 * 192 * 2560 * 512, bytes_accessed=3_600_000, transcendentals=0
        ),
        name="adapter",
    )(info, *pieces, w)


def copy_weights(info, groups, w, sem):
    x, y = info[4], info[5]
    copies = []

    def place(ref, at, dy, dx, low):
        index = lax.rem(y + dy + 4, 4) * 4 + lax.rem(x + dx + 4, 4)
        rows = pl.multiple_of(index * KPART + low, KPART // 2)
        copies.append(
            pltpu.make_async_copy(
                ref.at[pl.ds(at, KPART // 2)], w.at[pl.ds(rows, KPART // 2)], sem
            )
        )

    for which, group in enumerate((groups[:5], groups[5:])):
        for far in range(4):
            for near in range(4):
                at = near * (KPART // 2)
                ref = group[far]
                if far == 3 and near >= 2:
                    ref, at = group[4], at - KPART
                dy, dx = RING[far], RING[near]
                if which == 1:
                    dy, dx = dx, dy
                place(ref, at, dy, dx, which * (KPART // 2))
    return copies


def project(info, gain_ref, rows, xs, w, scale, emit):
    tile = 96

    def scale_rows(step, _):
        at = pl.ds(pl.multiple_of(step * tile, 16), tile)
        values = xs[at, :].astype(F32)
        scale[at, :] = lax.rsqrt(jnp.mean(values * values, axis=1, keepdims=True) + 1e-05)
        xs[at, :] = (values * gain_ref[...]).astype(BF)
        return 0

    lax.fori_loop(0, rows // tile, scale_rows, 0)

    def columns(at, width):
        both = jnp.dot(xs[...], w[:, at], preferred_element_type=F32) * scale[...]
        gate, up = both[:, :width], both[:, width:]
        return gate * (1.0 / (1.0 + jnp.exp(-gate))) * up

    def step(j, _):
        at = pl.ds(pl.multiple_of(j * 256, 256), 256)
        emit(pl.ds(pl.multiple_of(j * 128, 128), 128), columns(at, 128))
        return 0

    lax.fori_loop(0, 5, step, 0)
    emit(pl.ds(640, 48), columns(pl.ds(1280, 96), 48))


def text_kernel(info, gain_ref, *refs):
    groups, own, other = refs[:10], refs[10:18], refs[18]
    out_ref, xs, w, scale, sems = refs[19:]
    z, s = info[0], info[1]
    copies = copy_weights(info, groups, w, sems.at[0])
    for d in range(8):
        peer = lax.rem(z + d, 8)
        for part, ref in ((s, own[d]), (1 - s, other.at[d])):
            cols = pl.multiple_of((part * 8 + peer) * KPART, KPART)
            copies.append(pltpu.make_async_copy(ref, xs.at[:, pl.ds(cols, KPART)], sems.at[1]))
    for copy in copies:
        copy.start()
    for copy in copies:
        copy.wait()

    def emit(at, value):
        out_ref[:, at] = value.astype(BF)

    project(info, gain_ref, L_DEV, xs, w, scale, emit)


def text_hidden(info, gain, groups, own, other):
    return pl.pallas_call(
        text_kernel,
        out_shape=jax.ShapeDtypeStruct((L_DEV, FPART), BF),
        in_specs=[smem(), vmem()] + [hbm()] * 19,
        out_specs=vmem(),
        scratch_shapes=[
            pltpu.VMEM((L_DEV, D), BF),
            pltpu.VMEM((D, 2 * FPART), BF),
            pltpu.VMEM((L_DEV, 1), F32),
            pltpu.SemaphoreType.DMA((2,)),
        ],
        compiler_params=pltpu.CompilerParams(vmem_limit_bytes=40 * 1024 * 1024),
        cost_estimate=pl.CostEstimate(
            flops=2 * L_DEV * D * 2 * FPART, bytes_accessed=20_000_000, transcendentals=0
        ),
        name="text_hidden",
    )(info, gain, *groups, *own, other)


def speech_kernel(info, gain_ref, *refs):
    groups, own, other, text_ref = refs[:10], refs[10:18], refs[18], refs[19]
    out_ref, xs, w, scale, sems = refs[20:]
    z, s = info[0], info[1]
    copies = copy_weights(info, groups, w, sems.at[0])
    for d in range(8):
        peer = lax.rem(z + d, 8)
        for part, ref in ((s, own[d]), (1 - s, other.at[d])):
            rows = pl.ds(pl.multiple_of(part * 2 * MAXROWS, 2 * MAXROWS), 2 * MAXROWS)
            for half in range(2):
                cols = pl.multiple_of((half * 8 + peer) * KPART, KPART)
                copies.append(
                    pltpu.make_async_copy(
                        ref.at[:, pl.ds(half * KPART, KPART)],
                        xs.at[rows, pl.ds(cols, KPART)],
                        sems.at[1],
                    )
                )
    for copy in copies:
        copy.start()
    for copy in copies:
        copy.wait()
    row = lax.broadcasted_iota(jnp.int32, (REGION, MAXROWS), 0)
    slot_row = lax.broadcasted_iota(jnp.int32, (REGION, MAXROWS), 1)
    row_alone = lax.broadcasted_iota(jnp.int32, (REGION, 1), 0)

    def emit(at, value):
        value = value.astype(BF)
        for k in range(4):
            offset, length = info[8 + k], info[12 + k]
            pick = ((row - offset == slot_row) & (slot_row < length)).astype(BF)
            placed = jnp.dot(
                pick, value[k * MAXROWS : (k + 1) * MAXROWS], preferred_element_type=F32
            ).astype(BF)
            inside = (row_alone >= offset) & (row_alone < offset + length)
            here = slice(k * REGION, (k + 1) * REGION)
            out_ref[here, at] = jnp.where(inside, placed, text_ref[here, at])

    project(info, gain_ref, P_DEV, xs, w, scale, emit)


def speech_hidden(info, gain, groups, own, other, text):
    return pl.pallas_call(
        speech_kernel,
        out_shape=jax.ShapeDtypeStruct((L_DEV, FPART), BF),
        in_specs=[smem(), vmem()] + [hbm()] * 19 + [vmem()],
        out_specs=vmem(),
        scratch_shapes=[
            pltpu.VMEM((P_DEV, D), BF),
            pltpu.VMEM((D, 2 * FPART), BF),
            pltpu.VMEM((P_DEV, 1), F32),
            pltpu.SemaphoreType.DMA((2,)),
        ],
        compiler_params=pltpu.CompilerParams(vmem_limit_bytes=40 * 1024 * 1024),
        cost_estimate=pl.CostEstimate(
            flops=2 * P_DEV * D * 2 * FPART, bytes_accessed=20_000_000, transcendentals=0
        ),
        name="speech_hidden",
    )(info, gain, *groups, *own, other, text)


def gather_weights(gate_w, up_w):
    columns = []
    for j in range(5):
        columns += [gate_w[:, j * 128 : (j + 1) * 128], up_w[:, j * 128 : (j + 1) * 128]]
    columns += [gate_w[:, 640:], up_w[:, 640:]]
    packed = jnp.concatenate(columns, 1)
    groups = []
    halves = packed[: KPART // 2], packed[KPART // 2 :]
    for half, near, far in ((halves[0], shift_x, shift_y), (halves[1], shift_y, shift_x)):
        joined = jnp.concatenate(ring4(half, near), 0)
        groups += list(ring4(joined, far))
    return groups


def per_device(
    mel_frames,
    utt_rows,
    utt_owner,
    utt_offset,
    conv1_w,
    conv2_w,
    adapter_w,
    text_rows,
    norm_gain,
    gate_w,
    up_w,
):
    s, dp, z = lax.axis_index("section"), lax.axis_index("dp"), lax.axis_index("mp")
    x, y = lax.rem(dp, 4), lax.div(dp, 4)
    utts = jnp.arange(64, dtype=jnp.int32)
    earlier = (utt_owner[None, :] == utt_owner[:, None]) & (utts[None, :] < utts[:, None])
    starts = jnp.sum(jnp.where(earlier, utt_rows[None, :], 0), axis=1)

    mine = jnp.where(utt_owner == dp, starts, P_DEV).reshape(N_DP, 4)
    range_first = jnp.min(mine, axis=1)
    wanted = (range_first[:, None] + jnp.arange(MAXROWS, dtype=jnp.int32)[None, :]).reshape(-1)
    pooled = jnp.arange(P_DEV, dtype=jnp.int32)
    quads = mel_frames.reshape(P_DEV, 4 * MELS)
    send = jnp.dot(
        (wanted[:, None] == pooled[None, :]).astype(BF), quads, preferred_element_type=F32
    ).astype(BF)
    received = lax.all_to_all(send, "dp", 0, 0, tiled=True)

    def block(values):
        return lax.dynamic_slice_in_dim(values, dp * 4, 4, 0)

    lengths, owners, first = block(utt_rows), block(utt_owner), block(starts)
    offsets = block(utt_offset) - (dp * 4 + jnp.arange(4, dtype=jnp.int32)) * REGION
    block_first = jnp.min(
        jnp.where(owners[None, :] == owners[:, None], first[None, :], P_DEV), axis=1
    )
    at = owners * MAXROWS + first - block_first
    two = lax.dynamic_slice_in_dim(at, s * 2, 2, 0)
    two_len = lax.dynamic_slice_in_dim(lengths, s * 2, 2, 0)
    slot_row = jnp.arange(MAXROWS, dtype=jnp.int32)
    source = jnp.where(
        slot_row[None, :] < two_len[:, None], two[:, None] + slot_row[None, :], -1
    ).reshape(-1)
    every = jnp.arange(N_DP * MAXROWS, dtype=jnp.int32)
    slots = jnp.dot(
        (source[:, None] == every[None, :]).astype(BF), received, preferred_element_type=F32
    ).astype(BF)
    info = jnp.concatenate(
        [jnp.stack([z, s]), two_len, jnp.stack([x, y, y, y]), offsets, lengths]
    ).astype(jnp.int32)

    w1 = jnp.stack(direct_z(conv1_w.T))
    w1_other = swap(w1)
    w2_other = swap(conv2_w)
    w2 = jnp.concatenate(
        [jnp.where(s == 0, conv2_w, w2_other), jnp.where(s == 0, w2_other, conv2_w)], 1
    )
    wa_other = swap(adapter_w)
    wa = jnp.concatenate(
        [jnp.where(s == 0, adapter_w, wa_other), jnp.where(s == 0, wa_other, adapter_w)], 1
    )
    wa = wa.reshape(2, 2, 8, CPART, 2 * KPART).transpose(2, 0, 1, 3, 4)
    wa = wa.reshape(8, 4 * CPART, 2 * KPART)

    groups = gather_weights(gate_w, up_w)
    text_own = ring_z(text_rows)
    text_other = swap(jnp.stack(text_own))
    gain = norm_gain.reshape(1, D)

    maps = encoder(info, slots, w1, w1_other, w2)
    speech = adapter(info, ring_z(maps), wa)
    speech_own = ring_z(speech)
    speech_other = swap(jnp.stack(speech_own))
    text = text_hidden(info, gain, groups, text_own, text_other)
    return speech_hidden(info, gain, groups, speech_own, speech_other, text)


def solution(mesh):
    cols = ("section", "mp")
    return jax.shard_map(
        per_device,
        mesh=mesh,
        in_specs=(
            P("dp", None),
            P(),
            P(),
            P(),
            P(None, cols),
            P(None, cols),
            P(None, cols),
            P("dp", cols),
            P(),
            P("dp", cols),
            P("dp", cols),
        ),
        out_specs=P("dp", cols),
        check_vma=False,
    )
```

```python
import functools

import jax
import jax.numpy as jnp
from jax import lax
from jax.experimental import pallas as pl
from jax.experimental.pallas import tpu as pltpu
from jax.sharding import PartitionSpec as P

MELS = 128
C = 1280
D = 4096
N_DP = 16
MAXROWS = 96
ROWS = 2 * MAXROWS
P_DEV = 384
L_DEV = 768
REGION = 192
CPART = 80
FPART = 688
KPART = 256
BF = jnp.bfloat16
F32 = jnp.float32
MIB = 1024 * 1024
NT = (((1,), (1,)), ((), ()))


def step_x(a):
    return lax.ppermute(
        a,
        ("section", "dp"),
        [
            (c * 16 + y * 4 + x, c * 16 + y * 4 + (x + (1, 3)[c]) % 4)
            for c in range(2)
            for y in range(4)
            for x in range(4)
        ],
    )


def step_y(a):
    return lax.ppermute(
        a,
        ("section", "dp"),
        [
            (c * 16 + y * 4 + x, c * 16 + ((y + (1, 3)[c]) % 4) * 4 + x)
            for c in range(2)
            for y in range(4)
            for x in range(4)
        ],
    )


def step_z(a, k=1):
    return lax.ppermute(
        a,
        ("section", "mp"),
        [(c * 8 + z, c * 8 + (z + (k, 8 - k)[c]) % 8) for c in range(2) for z in range(8)],
    )


def shift_z(a, step):
    return lax.ppermute(a, "mp", [(i, (i + step) % 8) for i in range(8)])


def swap(a):
    return lax.ppermute(a, "section", [(0, 1), (1, 0)])


def gelu(v):
    return 0.5 * v * (1.0 + lax.erf(v * (0.5**0.5)))


def vmem():
    return pl.BlockSpec(memory_space=pltpu.VMEM)


def smem():
    return pl.BlockSpec(memory_space=pltpu.SMEM)


def hbm():
    return pl.BlockSpec(memory_space=pl.ANY)


def pack_kernel(info, utt_rows, utt_owner, quads_ref, out_ref, first):
    dp = info[2]

    def clear(b, _):
        first[b] = P_DEV
        return 0

    lax.fori_loop(0, N_DP, clear, 0)

    def look(u, start):
        own = utt_owner[u] == dp
        b = lax.div(u, 4)
        first[b] = jnp.where(own, jnp.minimum(first[b], start), first[b])
        return start + jnp.where(own, utt_rows[u], 0)

    lax.fori_loop(0, 64, look, jnp.int32(0))
    wanted = lax.broadcasted_iota(jnp.int32, (MAXROWS, P_DEV), 0)
    held = lax.broadcasted_iota(jnp.int32, (MAXROWS, P_DEV), 1)

    def block(b, _):
        pick = (wanted + first[b] == held).astype(BF)
        rows = pl.ds(pl.multiple_of(b * MAXROWS, 16), MAXROWS)
        out_ref[rows, :] = jnp.dot(pick, quads_ref[...], preferred_element_type=F32).astype(BF)
        return 0

    lax.fori_loop(0, N_DP, block, 0)


def pack(info, utt_rows, utt_owner, quads):
    return pl.pallas_call(
        pack_kernel,
        out_shape=jax.ShapeDtypeStruct((N_DP * MAXROWS, 4 * MELS), BF),
        in_specs=[smem(), smem(), smem(), vmem()],
        out_specs=vmem(),
        scratch_shapes=[pltpu.SMEM((N_DP,), jnp.int32)],
        compiler_params=pltpu.CompilerParams(vmem_limit_bytes=16 * MIB),
        cost_estimate=pl.CostEstimate(
            flops=2 * 1536 * 384 * 512, bytes_accessed=2_000_000, transcendentals=0
        ),
        name="pack",
    )(info, utt_rows, utt_owner, quads)


def encoder_kernel(
    info,
    utt_rows,
    utt_owner,
    received_ref,
    pair_ref,
    ahead_ref,
    behind_ref,
    w2a_ref,
    w2b_ref,
    out_ref,
    w1,
    y,
):
    z, s, dp = info[0], info[1], info[2]

    def place(part, peer, value):
        w1[pl.ds(pl.multiple_of((part * 8 + peer) * CPART, 16), CPART), :] = value

    for i in range(2):
        part = jnp.where(s == i, 0, 1)
        place(part, z, pair_ref[i])
        for k, hop in enumerate((1, 2, 3, 4)):
            step = jnp.where(s == 0, 8 - hop, hop)
            place(part, lax.rem(z + step, 8), ahead_ref[2 * k + i])
            place(1 - part, lax.rem(z + 8 - step, 8), behind_ref[2 * k + i])

    row = lax.broadcasted_iota(jnp.int32, (ROWS, 1), 0)
    slot_row = jnp.where(row < MAXROWS, row, row - MAXROWS)
    source = jnp.full((ROWS, 1), -1, jnp.int32)
    for slot in range(2):
        u = dp * 4 + s * 2 + slot
        owner = utt_owner[u]
        at = owner * MAXROWS
        for earlier in range(4):
            v = dp * 4 + earlier
            at += jnp.where((v < u) & (utt_owner[v] == owner), utt_rows[v], 0)
        here = (row >= slot * MAXROWS) & (row < (slot + 1) * MAXROWS) & (slot_row < utt_rows[u])
        source = jnp.where(here, at + slot_row, source)
    active = source >= 0
    every = lax.broadcasted_iota(jnp.int32, (ROWS, N_DP * MAXROWS), 1)
    x = jnp.dot(
        (source == every).astype(BF), received_ref[...], preferred_element_type=F32
    ).astype(BF)

    head = x[:, :MELS].astype(F32)
    tail = x[:, 3 * MELS :].astype(F32)
    before = jnp.where(slot_row == 0, 0.0, pltpu.roll(tail, 1, 0)).astype(BF)
    following = jnp.where(
        slot_row == MAXROWS - 1, 0.0, pltpu.roll(head, ROWS - 1, 0)
    ).astype(BF)
    wide = jnp.concatenate([before, x, following], 1)
    for tile in range(C // 256):
        weight = w1[tile * 256 : (tile + 1) * 256, :]
        for q in range(4):
            total = lax.dot_general(
                wide[:, q * MELS : (q + 3) * MELS], weight, NT, preferred_element_type=F32
            )
            y[q, :, tile * 256 : (tile + 1) * 256] = jnp.where(active, gelu(total), 0.0).astype(BF)
    last = y[3].astype(F32)
    y_before = jnp.where(slot_row == 0, 0.0, pltpu.roll(last, 1, 0)).astype(BF)
    dot = functools.partial(lax.dot_general, dimension_numbers=NT, preferred_element_type=F32)

    def second(ref):
        w_before, w_mid, w_after = ref[:, :C], ref[:, C : 2 * C], ref[:, 2 * C :]
        even = dot(y_before, w_before) + dot(y[0], w_mid) + dot(y[1], w_after)
        odd = dot(y[1], w_before) + dot(y[2], w_mid) + dot(y[3], w_after)
        return even, odd

    mine, others = second(w2a_ref), second(w2b_ref)
    parts = []
    for h in range(2):
        parts += [jnp.where(s == 0, mine[h], others[h]), jnp.where(s == 0, others[h], mine[h])]
    both = jnp.concatenate(parts, 1)
    out_ref[...] = jnp.where(active, gelu(both), 0.0).astype(BF)


def encoder(info, utt_rows, utt_owner, *arrays):
    return pl.pallas_call(
        encoder_kernel,
        out_shape=jax.ShapeDtypeStruct((ROWS, 4 * CPART), BF),
        in_specs=[smem()] * 3 + [vmem()] * 6,
        out_specs=vmem(),
        scratch_shapes=[pltpu.VMEM((C, 3 * MELS), BF), pltpu.VMEM((4, ROWS, C), BF)],
        compiler_params=pltpu.CompilerParams(vmem_limit_bytes=24 * MIB),
        cost_estimate=pl.CostEstimate(
            flops=2 * 192 * 4 * (384 * C + 3840 * 80), bytes_accessed=5_000_000, transcendentals=0
        ),
        name="encoder",
    )(info, utt_rows, utt_owner, *arrays)


def adapter_kernel(info, *refs):
    pieces, wa_ref, wb_ref, out_ref = refs[:8], refs[8], refs[9], refs[10]
    z, s = info[0], info[1]
    totals = [jnp.zeros((ROWS, KPART), F32), jnp.zeros((ROWS, KPART), F32)]
    for d in range(8):
        piece = pieces[d][...]
        peer = lax.rem(z + d, 8)
        for i, ref in enumerate((wa_ref, wb_ref)):
            weight = jnp.concatenate(
                [ref[pl.ds(pl.multiple_of((8 * j + peer) * CPART, 16), CPART), :] for j in range(4)],
                0,
            )
            totals[i] += jnp.dot(piece, weight, preferred_element_type=F32)
    mine, others = totals
    out_ref[:, :KPART] = jnp.where(s == 0, mine, others).astype(BF)
    out_ref[:, KPART:] = jnp.where(s == 0, others, mine).astype(BF)


def adapter(info, pieces, wa, wb):
    return pl.pallas_call(
        adapter_kernel,
        out_shape=jax.ShapeDtypeStruct((ROWS, 2 * KPART), BF),
        in_specs=[smem()] + [vmem()] * 10,
        out_specs=vmem(),
        compiler_params=pltpu.CompilerParams(vmem_limit_bytes=24 * MIB),
        cost_estimate=pl.CostEstimate(
            flops=2 * 192 * 2560 * 512, bytes_accessed=3_600_000, transcendentals=0
        ),
        name="adapter",
    )(info, *pieces, wa, wb)


def weight_copies(info, groups, gate, up, sem):
    s, dp = info[1], info[2]
    x, y = lax.rem(dp, 4), lax.div(dp, 4)
    copies = []
    for far in range(4):
        for near in range(4):
            far_step = jnp.where(s == 0, 4 - far, far)
            near_step = jnp.where(s == 0, 4 - near, near)
            for ref, at, dy, dx in (
                (groups[far], gate, far_step, near_step),
                (groups[4 + far], up, near_step, far_step),
            ):
                chunk = lax.rem(y + dy, 4) * 4 + lax.rem(x + dx, 4)
                cols = pl.ds(pl.multiple_of(chunk * KPART, KPART), KPART)
                copies.append(pltpu.make_async_copy(ref.at[near], at.at[:, cols], sem))
    return copies


def normalize(gain_ref, rows, xs, out):
    tile = 96

    def step(i, _):
        at = pl.ds(pl.multiple_of(i * tile, 16), tile)
        values = xs[at, :].astype(F32)
        scale = lax.rsqrt(jnp.mean(values * values, axis=1, keepdims=True) + 1e-05)
        out[at, :] = (values * scale * gain_ref[...]).astype(BF)
        return 0

    lax.fori_loop(0, rows // tile, step, 0)


def gated(gate, up, at, x):
    g = lax.dot_general(gate[at, :], x[...], NT, preferred_element_type=F32)
    u = lax.dot_general(up[at, :], x[...], NT, preferred_element_type=F32)
    return (g * (1.0 / (1.0 + jnp.exp(-g))) * u).astype(BF)


def text_norm_kernel(info, gain_ref, *refs):
    own, other = refs[:8], refs[8:10]
    out_ref, xs, sem = refs[10:]
    z, s = info[0], info[1]
    rows = []
    for k in range(8):
        step = jnp.where(s == 0, 8 - k, k)
        sibling = other[k // 4].at[k % 4]
        for part, ref, way in ((s, own[k], step), (1 - s, sibling, 8 - step)):
            cols = pl.multiple_of((part * 8 + lax.rem(z + way, 8)) * KPART, KPART)
            rows.append(pltpu.make_async_copy(ref, xs.at[:, pl.ds(cols, KPART)], sem))
    for copy in rows:
        copy.start()
    for copy in rows:
        copy.wait()
    normalize(gain_ref, L_DEV, xs, out_ref)


def text_norm(info, gain, own, other):
    return pl.pallas_call(
        text_norm_kernel,
        out_shape=jax.ShapeDtypeStruct((L_DEV, D), BF),
        in_specs=[smem(), vmem()] + [hbm()] * 10,
        out_specs=vmem(),
        scratch_shapes=[pltpu.VMEM((L_DEV, D), BF), pltpu.SemaphoreType.DMA],
        compiler_params=pltpu.CompilerParams(vmem_limit_bytes=18 * MIB),
        cost_estimate=pl.CostEstimate(
            flops=10 * L_DEV * D, bytes_accessed=13_000_000, transcendentals=0
        ),
        name="text_norm",
    )(info, gain, *own, *other)


def place_kernel(info, *refs):
    groups, gate, up, sem = refs[:8], refs[8], refs[9], refs[10]
    copies = weight_copies(info, groups, gate, up, sem)
    for copy in copies:
        copy.start()
    for copy in copies:
        copy.wait()


def place_weights(info, groups):
    return pl.pallas_call(
        place_kernel,
        out_shape=[jax.ShapeDtypeStruct((FPART, D), BF)] * 2,
        in_specs=[smem()] + [hbm()] * 8,
        out_specs=[vmem()] * 2,
        scratch_shapes=[pltpu.SemaphoreType.DMA],
        compiler_params=pltpu.CompilerParams(vmem_limit_bytes=14 * MIB),
        cost_estimate=pl.CostEstimate(flops=0, bytes_accessed=22_000_000, transcendentals=0),
        name="place_weights",
    )(info, *groups)


def text_tile_kernel(at, gate_ref, up_ref, x_ref, out_ref):
    out_ref[...] = gated(gate_ref, up_ref, pl.ds(*at), x_ref)


def text_tile(at, gate, up, x):
    return pl.pallas_call(
        functools.partial(text_tile_kernel, at),
        out_shape=jax.ShapeDtypeStruct((at[1], L_DEV), BF),
        in_specs=[vmem()] * 3,
        out_specs=vmem(),
        compiler_params=pltpu.CompilerParams(vmem_limit_bytes=24 * MIB),
        cost_estimate=pl.CostEstimate(
            flops=4 * L_DEV * D * at[1], bytes_accessed=10_000_000, transcendentals=0
        ),
        name="text_tile",
    )(gate, up, x)


TILES = ((0, 256), (256, 256), (512, 176))


def speech_kernel(info, utt_rows, utt_offset, gain_ref, *refs):
    own, other = refs[:8], refs[8]
    gate, up, texts = refs[9], refs[10], refs[11:14]
    out_ref, xs, sem = refs[14:]
    z, s, dp = info[0], info[1], info[2]
    rows = []
    for d in range(8):
        peer = lax.rem(z + d, 8)
        for part, ref in ((s, own[d]), (1 - s, other.at[d])):
            at = pl.ds(pl.multiple_of(part * ROWS, ROWS), ROWS)
            for half in range(2):
                cols = pl.multiple_of((half * 8 + peer) * KPART, KPART)
                rows.append(
                    pltpu.make_async_copy(
                        ref.at[:, pl.ds(half * KPART, KPART)],
                        xs.at[at, pl.ds(cols, KPART)],
                        sem,
                    )
                )
    for copy in rows:
        copy.start()
    for copy in rows:
        copy.wait()
    normalize(gain_ref, P_DEV, xs, xs)
    row = lax.broadcasted_iota(jnp.int32, (1, L_DEV), 1)
    source = jnp.full((1, L_DEV), -1, jnp.int32)
    for k in range(4):
        u = dp * 4 + k
        first = utt_offset[u] - dp * L_DEV
        inside = (row >= first) & (row < first + utt_rows[u])
        source = jnp.where(inside, row - first + k * MAXROWS, source)
    slot_row = lax.broadcasted_iota(jnp.int32, (P_DEV, L_DEV), 0)
    pick = (slot_row == source).astype(BF)
    for (start, size), text_ref in zip(TILES, texts):
        at = pl.ds(start, size)
        placed = jnp.dot(gated(gate, up, at, xs), pick, preferred_element_type=F32).astype(BF)
        out_ref[at, :] = jnp.where(source >= 0, placed, text_ref[...])


def speech_hidden(info, utt_rows, utt_offset, gain, own, other, gate, up, texts):
    return pl.pallas_call(
        speech_kernel,
        out_shape=jax.ShapeDtypeStruct((FPART, L_DEV), BF),
        in_specs=[smem()] * 3 + [vmem()] + [hbm()] * 9 + [vmem()] * 5,
        out_specs=vmem(),
        scratch_shapes=[pltpu.VMEM((P_DEV, D), BF), pltpu.SemaphoreType.DMA],
        compiler_params=pltpu.CompilerParams(vmem_limit_bytes=26 * MIB),
        cost_estimate=pl.CostEstimate(
            flops=2 * P_DEV * D * 2 * FPART, bytes_accessed=20_000_000, transcendentals=0
        ),
        name="speech_hidden",
    )(info, utt_rows, utt_offset, gain, *own, other, gate, up, *texts)


def per_device(
    mel_frames,
    utt_rows,
    utt_owner,
    utt_offset,
    conv1_w,
    conv2_w,
    adapter_w,
    text_rows,
    norm_gain,
    gate_w,
    up_w,
):
    info = jnp.stack(
        [lax.axis_index("mp"), lax.axis_index("section"), lax.axis_index("dp"), 0]
    ).astype(jnp.int32)
    gate, up = [gate_w.T], [up_w.T]
    text = [text_rows]
    w1 = conv1_w.T
    w2 = conv2_w.T

    def stage(values, *others):
        return lax.optimization_barrier((*values, *others))[: len(values)]

    w1_other = swap(w1)
    gate.append(step_x(gate[0]))
    up.append(step_y(up[0]))
    sent = pack(info, utt_rows, utt_owner, mel_frames.reshape(P_DEV, 4 * MELS))
    received = lax.all_to_all(sent, "dp", 0, 0, tiled=True)
    text.append(step_z(text[0]))
    w2_other = swap(w2)
    pair = jnp.stack([w1, w1_other])

    one, four, g, u, t, wa = stage(
        (pair, pair, gate[1], up[1], text[1], adapter_w), sent, w2_other
    )
    first = step_z(one, 1)
    gate.append(step_x(g))
    up.append(step_y(u))
    fourth = step_z(four, 4)
    text.append(step_z(t))

    double, g, u, t, wa = stage(
        (jnp.concatenate([pair, first], 0), gate[2], up[2], text[2], adapter_w), fourth
    )
    middle = step_z(double, 2)
    gate.append(step_x(g))
    up.append(step_y(u))
    text.append(step_z(t))
    wa_other = swap(wa)

    ahead = jnp.concatenate([first, middle, fourth], 0)
    ahead, t = stage((ahead, text[3]), gate[3], up[3])
    behind = swap(ahead)
    text.append(step_z(t))
    g, u = stage((jnp.stack(gate), jnp.stack(up)), received, wa_other)
    gates, ups = [g], [u]
    gates.append(step_y(g))
    ups.append(step_x(u))

    maps = encoder(info, utt_rows, utt_owner, received, pair, ahead, behind, w2, w2_other)

    def hop(forth, back, *others):
        forth, back = stage((forth, back), *others)
        return shift_z(forth, 1), shift_z(back, 7)

    def last_hop(forth, back, *others):
        half = forth.shape[0] // 2
        return jnp.concatenate(hop(forth[:half], back[half:], *others), 0)

    def by_offset(a, hops, last):
        return [a, hops[0][1], hops[1][1], hops[2][1], last, hops[2][0], hops[1][0], hops[0][0]]

    m1 = hop(maps, maps)
    (t,) = stage((text[4],), maps)
    text.append(step_z(t))
    m2 = hop(*m1)
    m3 = hop(*m2, text[5], gates[1], ups[1])
    g, u, t = stage((gates[1], ups[1], text[5]), *m2)
    gates.append(step_y(g))
    ups.append(step_x(u))
    text.append(step_z(t))
    m4 = last_hop(*m3)
    speech = adapter(info, by_offset(maps, (m1, m2, m3), m4), adapter_w, wa_other)

    s1 = hop(speech, speech, text[6])
    g, u, t = stage((gates[2], ups[2], text[6]), speech)
    text.append(step_z(t))
    gates.append(step_y(g))
    ups.append(step_x(u))
    s2 = hop(*s1, text[7])
    near, far = stage((jnp.stack(text[:4]), jnp.stack(text[4:])), *s1)
    others = [swap(near), swap(far)]
    gain = norm_gain.reshape(1, D)
    normed = text_norm(info, gain, text, others)
    s3 = hop(*s2, *others)
    forth, back = stage(s3, normed)
    s4 = last_hop(forth, back, gates[3], ups[3])
    weights = place_weights(info, gates + ups)
    texts = [text_tile(TILES[0], *weights, normed)]
    speech_own = by_offset(speech, (s1, s2, s3), s4)
    (whole,) = stage((jnp.stack(speech_own),), texts[0])
    speech_other = swap(whole)
    texts += [text_tile(at, *weights, normed) for at in TILES[1:]]
    out = speech_hidden(
        info, utt_rows, utt_offset, gain, speech_own, speech_other, *weights, texts
    )
    return out.T


def solution(mesh):
    cols = ("section", "mp")
    return jax.shard_map(
        per_device,
        mesh=mesh,
        in_specs=(
            P("dp", None),
            P(),
            P(),
            P(),
            P(None, cols),
            P(None, cols),
            P(None, cols),
            P("dp", cols),
            P(),
            P("dp", cols),
            P("dp", cols),
        ),
        out_specs=P("dp", cols),
        check_vma=False,
    )
```

```python
import functools

import jax
import jax.numpy as jnp
from jax import lax
from jax.experimental import pallas as pl
from jax.experimental.pallas import tpu as pltpu
from jax.sharding import PartitionSpec as P

MELS = 128
C = 1280
D = 4096
N_DP = 16
MAXROWS = 96
ROWS = 2 * MAXROWS
P_DEV = 384
L_DEV = 768
HALF = MAXROWS // 2
TEXT_REGION = 144
TEXT = 4 * TEXT_REGION
REGION = 192
CPART = 80
FPART = 688
KPART = 256
BF = jnp.bfloat16
F32 = jnp.float32
MIB = 1024 * 1024
NT = (((1,), (1,)), ((), ()))


def step_z(a, k=1):
    return lax.ppermute(
        a,
        ("section", "mp"),
        [(c * 8 + z, c * 8 + (z + (k, 8 - k)[c]) % 8) for c in range(2) for z in range(8)],
    )


def shift_z(a, step):
    return lax.ppermute(a, "mp", [(i, (i + step) % 8) for i in range(8)])


def swap(a):
    return lax.ppermute(a, "section", [(0, 1), (1, 0)])


def gelu(v):
    return 0.5 * v * (1.0 + lax.erf(v * (0.5**0.5)))


def vmem():
    return pl.BlockSpec(memory_space=pltpu.VMEM)


def smem():
    return pl.BlockSpec(memory_space=pltpu.SMEM)


def anywhere():
    return pl.BlockSpec(memory_space=pl.ANY)


def hbm():
    return pl.BlockSpec(memory_space=pltpu.HBM)


ROWS_AT, OWNER_AT, OFFSET_AT = 8, 72, 136


def pack_kernel(info, quads_ref, out_ref, pick, first):
    s, dp = info[1], info[2]
    for b in range(N_DP):
        first[b] = P_DEV

    def look(b, start):
        for i in range(4):
            own = info[OWNER_AT + 4 * b + i] == dp
            first[b] = jnp.where(own, jnp.minimum(first[b], start), first[b])
            start += jnp.where(own, info[ROWS_AT + 4 * b + i], 0)
        return start

    lax.fori_loop(0, N_DP, look, jnp.int32(0))
    wanted = lax.broadcasted_iota(jnp.int32, (HALF, P_DEV), 0) + s * HALF
    held = lax.broadcasted_iota(jnp.int32, (HALF, P_DEV), 1)
    for b in range(N_DP):
        pick[b * HALF : (b + 1) * HALF, :] = (wanted + first[b] == held).astype(BF)
    out_ref[...] = jnp.dot(pick[...], quads_ref[...], preferred_element_type=F32).astype(BF)


def pack(info, quads):
    return pl.pallas_call(
        pack_kernel,
        out_shape=jax.ShapeDtypeStruct((N_DP * HALF, 4 * MELS), BF),
        in_specs=[smem(), vmem()],
        out_specs=vmem(),
        scratch_shapes=[
            pltpu.VMEM((N_DP * HALF, P_DEV), BF),
            pltpu.SMEM((N_DP,), jnp.int32),
        ],
        compiler_params=pltpu.CompilerParams(vmem_limit_bytes=16 * MIB),
        cost_estimate=pl.CostEstimate(
            flops=2 * 1536 * 384 * 512, bytes_accessed=2_000_000, transcendentals=0
        ),
        name="pack",
    )(info, quads)


def load_kernel(info, text_ref, w1_ref, w1_other_ref, out_ref):
    dp = info[2]
    compact = lax.broadcasted_iota(jnp.int32, (TEXT_REGION, REGION), 0)
    packed = lax.broadcasted_iota(jnp.int32, (TEXT_REGION, REGION), 1)
    for k in range(4):
        u = dp * 4 + k
        offset = info[OFFSET_AT + u] - u * REGION
        source = compact + jnp.where(compact >= offset, info[ROWS_AT + u], 0)
        out_ref[k * TEXT_REGION : (k + 1) * TEXT_REGION, :] = jnp.dot(
            (source == packed).astype(BF),
            text_ref[k * REGION : (k + 1) * REGION, :],
            preferred_element_type=F32,
        ).astype(BF)
    for i, ref in enumerate((w1_ref, w1_other_ref)):
        at = TEXT + i * CPART
        out_ref[at : at + CPART, :] = ref[:, : 2 * MELS]
        out_ref[TEXT + 2 * CPART :, i * MELS : (i + 1) * MELS] = ref[:, 2 * MELS :]


def load_rows(info, text, w1, w1_other):
    return pl.pallas_call(
        load_kernel,
        out_shape=jax.ShapeDtypeStruct((TEXT + 3 * CPART, KPART), BF),
        in_specs=[smem()] + [vmem()] * 3,
        out_specs=vmem(),
        compiler_params=pltpu.CompilerParams(vmem_limit_bytes=16 * MIB),
        cost_estimate=pl.CostEstimate(
            flops=2 * TEXT * REGION * KPART, bytes_accessed=1_000_000, transcendentals=0
        ),
        name="load_rows",
    )(info, text, w1, w1_other)


def encoder_kernel(info, received_ref, received_other_ref, *refs):
    loads, w2a_hbm, w2b_hbm = refs[:8], refs[8], refs[9]
    out_ref, w1, y, w2a_ref, w2b_ref, loaded, sems = refs[10:]
    sem = sems.at[0]
    rows_in = [
        pltpu.make_async_copy(loads[d].at[pl.ds(TEXT, 3 * CPART)], loaded.at[d], sems.at[1])
        for d in range(8)
    ]
    for copy in rows_in:
        copy.start()
    fetches = [
        pltpu.make_async_copy(w2a_hbm, w2a_ref, sem),
        pltpu.make_async_copy(w2b_hbm, w2b_ref, sem),
    ]
    for fetch in fetches:
        fetch.start()
    z, s, dp = info[0], info[1], info[2]

    for copy in rows_in:
        copy.wait()
    for d in range(8):
        peer = lax.rem(z + d, 8)
        for i in range(2):
            part = jnp.where(s == i, 0, 1)
            at = pl.ds(pl.multiple_of((part * 8 + peer) * CPART, 16), CPART)
            w1[at, : 2 * MELS] = loaded[d, i * CPART : (i + 1) * CPART, :]
            w1[at, 2 * MELS :] = loaded[d, 2 * CPART :, i * MELS : (i + 1) * MELS]

    row = lax.broadcasted_iota(jnp.int32, (ROWS, 1), 0)
    slot_row = jnp.where(row < MAXROWS, row, row - MAXROWS)
    source = jnp.full((ROWS, 1), -1, jnp.int32)
    part = jnp.zeros((ROWS, 1), jnp.int32)
    for slot in range(2):
        u = dp * 4 + s * 2 + slot
        owner = info[OWNER_AT + u]
        at = jnp.int32(0)
        for earlier in range(4):
            v = dp * 4 + earlier
            at += jnp.where((v < u) & (info[OWNER_AT + v] == owner), info[ROWS_AT + v], 0)
        here = (row >= slot * MAXROWS) & (row < (slot + 1) * MAXROWS) & (slot_row < info[ROWS_AT + u])
        late = at + slot_row >= HALF
        source = jnp.where(
            here, owner * HALF + at + slot_row - jnp.where(late, HALF, 0), source
        )
        part = jnp.where(here & late, 1, part)
    active = source >= 0
    every = lax.broadcasted_iota(jnp.int32, (ROWS, N_DP * HALF), 1)
    x = (
        jnp.dot(
            (jnp.where(part == s, source, -1) == every).astype(BF),
            received_ref[...],
            preferred_element_type=F32,
        )
        + jnp.dot(
            (jnp.where(part == s, -1, source) == every).astype(BF),
            received_other_ref[...],
            preferred_element_type=F32,
        )
    ).astype(BF)

    head = x[:, :MELS].astype(F32)
    tail = x[:, 3 * MELS :].astype(F32)
    before = jnp.where(slot_row == 0, 0.0, pltpu.roll(tail, 1, 0)).astype(BF)
    following = jnp.where(
        slot_row == MAXROWS - 1, 0.0, pltpu.roll(head, ROWS - 1, 0)
    ).astype(BF)
    wide = jnp.concatenate([before, x, following], 1)
    for tile in range(C // 256):
        weight = w1[tile * 256 : (tile + 1) * 256, :]
        for q in range(4):
            total = lax.dot_general(
                wide[:, q * MELS : (q + 3) * MELS], weight, NT, preferred_element_type=F32
            )
            y[q, :, tile * 256 : (tile + 1) * 256] = jnp.where(active, gelu(total), 0.0).astype(BF)
    last = y[3].astype(F32)
    y_before = jnp.where(slot_row == 0, 0.0, pltpu.roll(last, 1, 0)).astype(BF)
    dot = functools.partial(lax.dot_general, dimension_numbers=NT, preferred_element_type=F32)
    for fetch in fetches:
        fetch.wait()

    def second(ref):
        w_before, w_mid, w_after = ref[:, :C], ref[:, C : 2 * C], ref[:, 2 * C :]
        even = dot(y_before, w_before) + dot(y[0], w_mid) + dot(y[1], w_after)
        odd = dot(y[1], w_before) + dot(y[2], w_mid) + dot(y[3], w_after)
        return even, odd

    mine, others = second(w2a_ref), second(w2b_ref)
    parts = []
    for h in range(2):
        parts += [jnp.where(s == 0, mine[h], others[h]), jnp.where(s == 0, others[h], mine[h])]
    both = jnp.concatenate(parts, 1)
    out_ref[...] = jnp.where(active, gelu(both), 0.0).astype(BF)


def encoder(info, *arrays):
    return pl.pallas_call(
        encoder_kernel,
        out_shape=jax.ShapeDtypeStruct((ROWS, 4 * CPART), BF),
        in_specs=[smem(), vmem(), vmem()] + [anywhere()] * 8 + [hbm()] * 2,
        out_specs=vmem(),
        scratch_shapes=[
            pltpu.VMEM((C, 3 * MELS), BF),
            pltpu.VMEM((4, ROWS, C), BF),
            pltpu.VMEM((CPART, 3 * C), BF),
            pltpu.VMEM((CPART, 3 * C), BF),
            pltpu.VMEM((8, 3 * CPART, 2 * MELS), BF),
            pltpu.SemaphoreType.DMA((2,)),
        ],
        compiler_params=pltpu.CompilerParams(vmem_limit_bytes=24 * MIB),
        cost_estimate=pl.CostEstimate(
            flops=2 * 192 * 4 * (384 * C + 3840 * 80), bytes_accessed=5_000_000, transcendentals=0
        ),
        name="encoder",
    )(info, *arrays)


def adapter_kernel(info, *refs):
    pieces, wa_ref, wb_ref, out_ref = refs[:8], refs[8], refs[9], refs[10]
    z, s = info[0], info[1]
    totals = [jnp.zeros((ROWS, KPART), F32), jnp.zeros((ROWS, KPART), F32)]
    for d in range(8):
        piece = pieces[d][...]
        peer = lax.rem(z + d, 8)
        for i, ref in enumerate((wa_ref, wb_ref)):
            weight = jnp.concatenate(
                [ref[pl.ds(pl.multiple_of((8 * j + peer) * CPART, 16), CPART), :] for j in range(4)],
                0,
            )
            totals[i] += jnp.dot(piece, weight, preferred_element_type=F32)
    mine, others = totals
    out_ref[:, :KPART] = jnp.where(s == 0, mine, others).astype(BF)
    out_ref[:, KPART:] = jnp.where(s == 0, others, mine).astype(BF)


def adapter(info, pieces, wa, wb):
    return pl.pallas_call(
        adapter_kernel,
        out_shape=jax.ShapeDtypeStruct((ROWS, 2 * KPART), BF),
        in_specs=[smem()] + [vmem()] * 10,
        out_specs=vmem(),
        compiler_params=pltpu.CompilerParams(vmem_limit_bytes=24 * MIB),
        cost_estimate=pl.CostEstimate(
            flops=2 * 192 * 2560 * 512, bytes_accessed=3_600_000, transcendentals=0
        ),
        name="adapter",
    )(info, *pieces, wa, wb)


def normalize(gain_ref, rows, xs, out):
    tile = 96

    def step(i, _):
        at = pl.ds(pl.multiple_of(i * tile, 16), tile)
        values = xs[at, :].astype(F32)
        scale = lax.rsqrt(jnp.mean(values * values, axis=1, keepdims=True) + 1e-05)
        out[at, :] = (values * scale * gain_ref[...]).astype(BF)
        return 0

    lax.fori_loop(0, rows // tile, step, 0)


def gated(gate, up, at, x):
    g = lax.dot_general(gate[at, :], x[...], NT, preferred_element_type=F32)
    u = lax.dot_general(up[at, :], x[...], NT, preferred_element_type=F32)
    return (g * (1.0 / (1.0 + jnp.exp(-g))) * u).astype(BF)


def text_norm_kernel(info, gain_ref, *refs):
    own, other = refs[:8], refs[8:16]
    out_ref, xs, sem = refs[16:]
    z, s = info[0], info[1]
    rows = []
    for d in range(8):
        peer = lax.rem(z + d, 8)
        for part, ref in ((s, own[d]), (1 - s, other[d])):
            cols = pl.multiple_of((part * 8 + peer) * KPART, KPART)
            rows.append(
                pltpu.make_async_copy(
                    ref.at[pl.ds(0, TEXT)], xs.at[:, pl.ds(cols, KPART)], sem
                )
            )
    for copy in rows:
        copy.start()
    for copy in rows:
        copy.wait()
    normalize(gain_ref, TEXT, xs, out_ref)


def text_norm(info, gain, own, other):
    return pl.pallas_call(
        text_norm_kernel,
        out_shape=jax.ShapeDtypeStruct((TEXT, D), BF),
        in_specs=[smem(), vmem()] + [anywhere()] * 16,
        out_specs=vmem(),
        scratch_shapes=[pltpu.VMEM((TEXT, D), BF), pltpu.SemaphoreType.DMA],
        compiler_params=pltpu.CompilerParams(vmem_limit_bytes=18 * MIB),
        cost_estimate=pl.CostEstimate(
            flops=10 * TEXT * D, bytes_accessed=10_000_000, transcendentals=0
        ),
        name="text_norm",
    )(info, gain, *own, *other)


def place_kernel(all_ref, gate, up, sem):
    copies = []
    for chunk in range(N_DP):
        cols = slice(chunk * KPART, (chunk + 1) * KPART)
        for i, ref in enumerate((gate, up)):
            copies.append(pltpu.make_async_copy(all_ref.at[chunk, i], ref.at[:, cols], sem))
    for copy in copies:
        copy.start()
    for copy in copies:
        copy.wait()


def place_weights(gathered):
    return pl.pallas_call(
        place_kernel,
        out_shape=[jax.ShapeDtypeStruct((FPART, D), BF)] * 2,
        in_specs=[hbm()],
        out_specs=[vmem()] * 2,
        scratch_shapes=[pltpu.SemaphoreType.DMA],
        compiler_params=pltpu.CompilerParams(vmem_limit_bytes=44 * MIB),
        cost_estimate=pl.CostEstimate(flops=0, bytes_accessed=22_000_000, transcendentals=0),
        name="place_weights",
    )(gathered)


def text_tile_kernel(at, info, gate_ref, up_ref, x_ref, out_ref):
    dp = info[2]
    row = lax.broadcasted_iota(jnp.int32, (1, L_DEV), 1)
    compact = jnp.full((1, L_DEV), -1, jnp.int32)
    for k in range(4):
        u = dp * 4 + k
        first = info[OFFSET_AT + u] - dp * L_DEV
        end = first + info[ROWS_AT + u]
        shift = k * (REGION - TEXT_REGION)
        region = (row >= k * REGION) & (row < (k + 1) * REGION)
        compact = jnp.where(region & (row < first), row - shift, compact)
        compact = jnp.where(region & (row >= end), row - shift - info[ROWS_AT + u], compact)
    place = (lax.broadcasted_iota(jnp.int32, (TEXT, L_DEV), 0) == compact).astype(BF)
    hidden = gated(gate_ref, up_ref, pl.ds(*at), x_ref)
    out_ref[...] = jnp.dot(hidden, place, preferred_element_type=F32).astype(BF)


def text_tile(at, info, gate, up, x):
    return pl.pallas_call(
        functools.partial(text_tile_kernel, at),
        out_shape=jax.ShapeDtypeStruct((at[1], L_DEV), BF),
        in_specs=[smem()] + [vmem()] * 3,
        out_specs=vmem(),
        compiler_params=pltpu.CompilerParams(vmem_limit_bytes=24 * MIB),
        cost_estimate=pl.CostEstimate(
            flops=4 * TEXT * D * at[1], bytes_accessed=10_000_000, transcendentals=0
        ),
        name="text_tile",
    )(info, gate, up, x)


TILES = ((0, 256), (256, 256), (512, 176))


def speech_rows(info, gain_ref, pieces, xs, sem):
    copies = []
    for d in range(8):
        peer = lax.rem(info[0] + d, 8)
        for half in range(2):
            cols = pl.multiple_of((half * 8 + peer) * KPART, KPART)
            copies.append(
                pltpu.make_async_copy(
                    pieces[d].at[:, pl.ds(half * KPART, KPART)], xs.at[:, pl.ds(cols, KPART)], sem
                )
            )
    for copy in copies:
        copy.start()
    for copy in copies:
        copy.wait()
    normalize(gain_ref, ROWS, xs, xs)


def own_kernel(info, gain_ref, *refs):
    pieces, gate, up, out_ref, xs, sem = refs[:8], *refs[8:]
    speech_rows(info, gain_ref, pieces, xs, sem)
    for tile in TILES:
        at = pl.ds(*tile)
        out_ref[at, :] = gated(gate, up, at, xs)


def own_hidden(info, gain, pieces, gate, up):
    return pl.pallas_call(
        own_kernel,
        out_shape=jax.ShapeDtypeStruct((FPART, ROWS), BF),
        in_specs=[smem(), vmem()] + [anywhere()] * 8 + [vmem()] * 2,
        out_specs=vmem(),
        scratch_shapes=[pltpu.VMEM((ROWS, D), BF), pltpu.SemaphoreType.DMA],
        compiler_params=pltpu.CompilerParams(vmem_limit_bytes=24 * MIB),
        cost_estimate=pl.CostEstimate(
            flops=2 * ROWS * D * 2 * FPART, bytes_accessed=14_000_000, transcendentals=0
        ),
        name="own_hidden",
    )(info, gain, *pieces, gate, up)


def speech_kernel(info, gain_ref, *refs):
    pieces, gate, up, own_ref, texts = refs[:8], refs[8], refs[9], refs[10], refs[11:14]
    out_ref, xs, sem = refs[14:]
    s, dp = info[1], info[2]
    speech_rows(info, gain_ref, pieces, xs, sem)
    row = lax.broadcasted_iota(jnp.int32, (1, L_DEV), 1)
    sources = []
    for part in (s, 1 - s):
        source = jnp.full((1, L_DEV), -1, jnp.int32)
        for slot in range(2):
            u = dp * 4 + part * 2 + slot
            first = info[OFFSET_AT + u] - dp * L_DEV
            inside = (row >= first) & (row < first + info[ROWS_AT + u])
            source = jnp.where(inside, row - first + slot * MAXROWS, source)
        sources.append(source)
    slot_row = lax.broadcasted_iota(jnp.int32, (ROWS, L_DEV), 0)
    picks = [(slot_row == source).astype(BF) for source in sources]
    speech = (sources[0] >= 0) | (sources[1] >= 0)
    for (start, size), text_ref in zip(TILES, texts):
        at = pl.ds(start, size)
        placed = jnp.dot(own_ref[at, :], picks[0], preferred_element_type=F32) + jnp.dot(
            gated(gate, up, at, xs), picks[1], preferred_element_type=F32
        )
        out_ref[at, :] = jnp.where(speech, placed.astype(BF), text_ref[...])


def speech_hidden(info, gain, pieces, gate, up, own, texts):
    return pl.pallas_call(
        speech_kernel,
        out_shape=jax.ShapeDtypeStruct((FPART, L_DEV), BF),
        in_specs=[smem(), vmem()] + [anywhere()] * 8 + [vmem()] * 6,
        out_specs=vmem(),
        scratch_shapes=[pltpu.VMEM((ROWS, D), BF), pltpu.SemaphoreType.DMA],
        compiler_params=pltpu.CompilerParams(vmem_limit_bytes=24 * MIB),
        cost_estimate=pl.CostEstimate(
            flops=2 * ROWS * D * 2 * FPART, bytes_accessed=16_000_000, transcendentals=0
        ),
        name="speech_hidden",
    )(info, gain, *pieces, gate, up, own, *texts)


def per_device(
    mel_frames,
    utt_rows,
    utt_owner,
    utt_offset,
    conv1_w,
    conv2_w,
    adapter_w,
    text_rows,
    norm_gain,
    gate_w,
    up_w,
):
    s = lax.axis_index("section")
    place = [lax.axis_index("mp"), s, lax.axis_index("dp")]
    info = jnp.concatenate(
        [jnp.stack(place + [0] * 5).astype(jnp.int32), utt_rows, utt_owner, utt_offset]
    )
    gathered = lax.all_gather(jnp.stack([gate_w.T, up_w.T]), "dp", axis=0)

    def stage(values, *others):
        return lax.optimization_barrier((*values, *others))[: len(values)]

    def hop(forth, back):
        return shift_z(forth, 1), shift_z(back, 7)

    def last_hop(forth, back):
        half = forth.shape[0] // 2
        return jnp.concatenate(hop(forth[:half], back[half:]), 0)

    def by_offset(a, hops, last):
        return [a, hops[0][1], hops[1][1], hops[2][1], last, hops[2][0], hops[1][0], hops[0][0]]

    w1 = conv1_w.T
    w1_other = swap(w1)

    sent = pack(info, mel_frames.reshape(P_DEV, 4 * MELS))
    received = lax.all_to_all(sent, "dp", 0, 0, tiled=True)
    load = load_rows(info, *stage((text_rows, w1, w1_other), sent))

    t1 = hop(load, load)
    w2, wa, own = stage((conv2_w.T, adapter_w, load), sent, *t1)
    w2_other, wa_other, load_other = swap(w2), swap(wa), swap(own)
    t2 = hop(*t1)
    o1 = [swap(v) for v in stage(t1, w2_other, wa_other, load_other)]
    t3 = hop(*stage(t2, w2_other, wa_other, load_other))
    o2 = [swap(v) for v in stage(t2, *o1)]
    forth, back = stage(t3, received, *o1)
    t4 = step_z(jnp.where(s == 0, forth, back))
    received_other = swap(received)
    maps = encoder(
        info, received, received_other, *by_offset(load, (t1, t2, t3), t4), w2, w2_other
    )

    m1 = hop(*stage((maps, maps), *o2))
    o3 = [swap(v) for v in stage((*t3, t4), maps)]
    m2 = hop(*m1)
    gain = norm_gain.reshape(1, D)
    text = stage(by_offset(load, (t1, t2, t3), t4), *m1)
    normed = text_norm(info, gain, text, by_offset(load_other, (o1, o2, o3), o3[2]))
    m3 = hop(*stage(m2, normed))
    m4 = last_hop(*m3)
    speech = adapter(info, by_offset(maps, (m1, m2, m3), m4), adapter_w, wa_other)

    s1 = hop(speech, speech)
    o0 = swap(speech)
    (here,) = stage((gathered,), speech)
    weights = place_weights(here)
    s2 = hop(*stage(s1, *weights))
    o1 = [swap(v) for v in stage(s1, o0)]
    texts = [text_tile(TILES[0], info, *weights, stage((normed,), *s1)[0])]
    s3 = hop(*stage(s2, *o1, texts[0]))
    o2 = [swap(v) for v in stage(s2, *o1)]
    texts.append(text_tile(TILES[1], info, *weights, stage((normed,), *s2)[0]))
    s4 = last_hop(*stage(s3, *o2, texts[1]))
    o3 = [swap(v) for v in stage(s3, *o2)]
    texts.append(text_tile(TILES[2], info, *weights, stage((normed,), *s3)[0]))
    (end,) = stage((s4,), *o3, *texts)
    o4 = swap(end)
    own = own_hidden(info, gain, by_offset(speech, (s1, s2, s3), end), *weights)
    other = by_offset(o0, (o1, o2, o3), o4)
    return speech_hidden(info, gain, other, *weights, own, texts).T


def solution(mesh):
    cols = ("section", "mp")
    return jax.shard_map(
        per_device,
        mesh=mesh,
        in_specs=(
            P("dp", None),
            P(),
            P(),
            P(),
            P(None, cols),
            P(None, cols),
            P(None, cols),
            P("dp", cols),
            P(),
            P("dp", cols),
            P("dp", cols),
        ),
        out_specs=P("dp", cols),
        check_vma=False,
    )
```

```python
import functools

import jax
import jax.numpy as jnp
from jax import lax
from jax.experimental import pallas as pl
from jax.experimental.pallas import tpu as pltpu
from jax.sharding import PartitionSpec as P

MELS = 128
C = 1280
D = 4096
N_DP = 16
MAXROWS = 96
ROWS = 2 * MAXROWS
P_DEV = 384
L_DEV = 768
HALF = MAXROWS // 2
TEXT_REGION = 144
TEXT = 4 * TEXT_REGION
REGION = 192
CPART = 80
FPART = 688
KPART = 256
BF = jnp.bfloat16
F32 = jnp.float32
MIB = 1024 * 1024
NT = (((1,), (1,)), ((), ()))


def step_z(a, k=1):
    return lax.ppermute(
        a,
        ("section", "mp"),
        [(c * 8 + z, c * 8 + (z + (k, 8 - k)[c]) % 8) for c in range(2) for z in range(8)],
    )


def shift_z(a, step):
    return lax.ppermute(a, "mp", [(i, (i + step) % 8) for i in range(8)])


def swap(a):
    return lax.ppermute(a, "section", [(0, 1), (1, 0)])


def gelu(v):
    return 0.5 * v * (1.0 + lax.erf(v * (0.5**0.5)))


def vmem():
    return pl.BlockSpec(memory_space=pltpu.VMEM)


def smem():
    return pl.BlockSpec(memory_space=pltpu.SMEM)


def anywhere():
    return pl.BlockSpec(memory_space=pl.ANY)


def hbm():
    return pl.BlockSpec(memory_space=pltpu.HBM)


ROWS_AT, OWNER_AT, OFFSET_AT = 8, 72, 136


def pack_kernel(info, quads_ref, out_ref, pick, first):
    s, dp = info[1], info[2]
    for b in range(N_DP):
        first[b] = P_DEV

    def look(b, start):
        for i in range(4):
            own = info[OWNER_AT + 4 * b + i] == dp
            first[b] = jnp.where(own, jnp.minimum(first[b], start), first[b])
            start += jnp.where(own, info[ROWS_AT + 4 * b + i], 0)
        return start

    lax.fori_loop(0, N_DP, look, jnp.int32(0))
    wanted = lax.broadcasted_iota(jnp.int32, (HALF, P_DEV), 0) + s * HALF
    held = lax.broadcasted_iota(jnp.int32, (HALF, P_DEV), 1)
    for b in range(N_DP):
        pick[b * HALF : (b + 1) * HALF, :] = (wanted + first[b] == held).astype(BF)
    out_ref[...] = jnp.dot(pick[...], quads_ref[...], preferred_element_type=F32).astype(BF)


def pack(info, quads):
    return pl.pallas_call(
        pack_kernel,
        out_shape=jax.ShapeDtypeStruct((N_DP * HALF, 4 * MELS), BF),
        in_specs=[smem(), vmem()],
        out_specs=vmem(),
        scratch_shapes=[
            pltpu.VMEM((N_DP * HALF, P_DEV), BF),
            pltpu.SMEM((N_DP,), jnp.int32),
        ],
        compiler_params=pltpu.CompilerParams(vmem_limit_bytes=16 * MIB),
        cost_estimate=pl.CostEstimate(
            flops=2 * 1536 * 384 * 512, bytes_accessed=2_000_000, transcendentals=0
        ),
        name="pack",
    )(info, quads)


def load_kernel(info, text_ref, w1_ref, w1_other_ref, out_ref):
    dp = info[2]
    compact = lax.broadcasted_iota(jnp.int32, (TEXT_REGION, REGION), 0)
    packed = lax.broadcasted_iota(jnp.int32, (TEXT_REGION, REGION), 1)
    for k in range(4):
        u = dp * 4 + k
        offset = info[OFFSET_AT + u] - u * REGION
        source = compact + jnp.where(compact >= offset, info[ROWS_AT + u], 0)
        out_ref[k * TEXT_REGION : (k + 1) * TEXT_REGION, :] = jnp.dot(
            (source == packed).astype(BF),
            text_ref[k * REGION : (k + 1) * REGION, :],
            preferred_element_type=F32,
        ).astype(BF)
    for i, ref in enumerate((w1_ref, w1_other_ref)):
        at = TEXT + i * CPART
        out_ref[at : at + CPART, :] = ref[:, : 2 * MELS]
        out_ref[TEXT + 2 * CPART :, i * MELS : (i + 1) * MELS] = ref[:, 2 * MELS :]


def load_rows(info, text, w1, w1_other):
    return pl.pallas_call(
        load_kernel,
        out_shape=jax.ShapeDtypeStruct((TEXT + 3 * CPART, KPART), BF),
        in_specs=[smem()] + [vmem()] * 3,
        out_specs=vmem(),
        compiler_params=pltpu.CompilerParams(vmem_limit_bytes=16 * MIB),
        cost_estimate=pl.CostEstimate(
            flops=2 * TEXT * REGION * KPART, bytes_accessed=1_000_000, transcendentals=0
        ),
        name="load_rows",
    )(info, text, w1, w1_other)


def encoder_kernel(info, received_ref, received_other_ref, *refs):
    loads, w2a_hbm, w2b_hbm = refs[:8], refs[8], refs[9]
    out_ref, w1, y, w2a_ref, w2b_ref, loaded, sems = refs[10:]
    sem = sems.at[0]
    rows_in = [
        pltpu.make_async_copy(loads[d].at[pl.ds(TEXT, 3 * CPART)], loaded.at[d], sems.at[1])
        for d in range(8)
    ]
    for copy in rows_in:
        copy.start()
    fetches = [
        pltpu.make_async_copy(w2a_hbm, w2a_ref, sem),
        pltpu.make_async_copy(w2b_hbm, w2b_ref, sem),
    ]
    for fetch in fetches:
        fetch.start()
    z, s, dp = info[0], info[1], info[2]

    for copy in rows_in:
        copy.wait()
    for d in range(8):
        peer = lax.rem(z + d, 8)
        for i in range(2):
            part = jnp.where(s == i, 0, 1)
            at = pl.ds(pl.multiple_of((part * 8 + peer) * CPART, 16), CPART)
            w1[at, : 2 * MELS] = loaded[d, i * CPART : (i + 1) * CPART, :]
            w1[at, 2 * MELS :] = loaded[d, 2 * CPART :, i * MELS : (i + 1) * MELS]

    row = lax.broadcasted_iota(jnp.int32, (ROWS, 1), 0)
    slot_row = jnp.where(row < MAXROWS, row, row - MAXROWS)
    source = jnp.full((ROWS, 1), -1, jnp.int32)
    part = jnp.zeros((ROWS, 1), jnp.int32)
    for slot in range(2):
        u = dp * 4 + s * 2 + slot
        owner = info[OWNER_AT + u]
        at = jnp.int32(0)
        for earlier in range(4):
            v = dp * 4 + earlier
            at += jnp.where((v < u) & (info[OWNER_AT + v] == owner), info[ROWS_AT + v], 0)
        here = (row >= slot * MAXROWS) & (row < (slot + 1) * MAXROWS) & (slot_row < info[ROWS_AT + u])
        late = at + slot_row >= HALF
        source = jnp.where(
            here, owner * HALF + at + slot_row - jnp.where(late, HALF, 0), source
        )
        part = jnp.where(here & late, 1, part)
    active = source >= 0
    every = lax.broadcasted_iota(jnp.int32, (ROWS, N_DP * HALF), 1)
    x = (
        jnp.dot(
            (jnp.where(part == s, source, -1) == every).astype(BF),
            received_ref[...],
            preferred_element_type=F32,
        )
        + jnp.dot(
            (jnp.where(part == s, -1, source) == every).astype(BF),
            received_other_ref[...],
            preferred_element_type=F32,
        )
    ).astype(BF)

    head = x[:, :MELS].astype(F32)
    tail = x[:, 3 * MELS :].astype(F32)
    before = jnp.where(slot_row == 0, 0.0, pltpu.roll(tail, 1, 0)).astype(BF)
    following = jnp.where(
        slot_row == MAXROWS - 1, 0.0, pltpu.roll(head, ROWS - 1, 0)
    ).astype(BF)
    wide = jnp.concatenate([before, x, following], 1)
    for tile in range(C // 256):
        weight = w1[tile * 256 : (tile + 1) * 256, :]
        for q in range(4):
            total = lax.dot_general(
                wide[:, q * MELS : (q + 3) * MELS], weight, NT, preferred_element_type=F32
            )
            y[q, :, tile * 256 : (tile + 1) * 256] = jnp.where(active, gelu(total), 0.0).astype(BF)
    last = y[3].astype(F32)
    y_before = jnp.where(slot_row == 0, 0.0, pltpu.roll(last, 1, 0)).astype(BF)
    dot = functools.partial(lax.dot_general, dimension_numbers=NT, preferred_element_type=F32)
    for fetch in fetches:
        fetch.wait()

    def second(ref):
        w_before, w_mid, w_after = ref[:, :C], ref[:, C : 2 * C], ref[:, 2 * C :]
        even = dot(y_before, w_before) + dot(y[0], w_mid) + dot(y[1], w_after)
        odd = dot(y[1], w_before) + dot(y[2], w_mid) + dot(y[3], w_after)
        return even, odd

    mine, others = second(w2a_ref), second(w2b_ref)
    parts = []
    for h in range(2):
        parts += [jnp.where(s == 0, mine[h], others[h]), jnp.where(s == 0, others[h], mine[h])]
    both = jnp.concatenate(parts, 1)
    out_ref[...] = jnp.where(active, gelu(both), 0.0).astype(BF)


def encoder(info, *arrays):
    return pl.pallas_call(
        encoder_kernel,
        out_shape=jax.ShapeDtypeStruct((ROWS, 4 * CPART), BF),
        in_specs=[smem(), vmem(), vmem()] + [anywhere()] * 8 + [hbm()] * 2,
        out_specs=vmem(),
        scratch_shapes=[
            pltpu.VMEM((C, 3 * MELS), BF),
            pltpu.VMEM((4, ROWS, C), BF),
            pltpu.VMEM((CPART, 3 * C), BF),
            pltpu.VMEM((CPART, 3 * C), BF),
            pltpu.VMEM((8, 3 * CPART, 2 * MELS), BF),
            pltpu.SemaphoreType.DMA((2,)),
        ],
        compiler_params=pltpu.CompilerParams(vmem_limit_bytes=24 * MIB),
        cost_estimate=pl.CostEstimate(
            flops=2 * 192 * 4 * (384 * C + 3840 * 80), bytes_accessed=5_000_000, transcendentals=0
        ),
        name="encoder",
    )(info, *arrays)


def adapter_kernel(info, *refs):
    pieces, wa_ref, wb_ref, out_ref = refs[:8], refs[8], refs[9], refs[10]
    z, s = info[0], info[1]
    totals = [jnp.zeros((ROWS, KPART), F32), jnp.zeros((ROWS, KPART), F32)]
    for d in range(8):
        piece = pieces[d][...]
        peer = lax.rem(z + d, 8)
        for i, ref in enumerate((wa_ref, wb_ref)):
            weight = jnp.concatenate(
                [ref[pl.ds(pl.multiple_of((8 * j + peer) * CPART, 16), CPART), :] for j in range(4)],
                0,
            )
            totals[i] += jnp.dot(piece, weight, preferred_element_type=F32)
    mine, others = totals
    out_ref[:, :KPART] = jnp.where(s == 0, mine, others).astype(BF)
    out_ref[:, KPART:] = jnp.where(s == 0, others, mine).astype(BF)


def adapter(info, pieces, wa, wb):
    return pl.pallas_call(
        adapter_kernel,
        out_shape=jax.ShapeDtypeStruct((ROWS, 2 * KPART), BF),
        in_specs=[smem()] + [vmem()] * 10,
        out_specs=vmem(),
        compiler_params=pltpu.CompilerParams(vmem_limit_bytes=24 * MIB),
        cost_estimate=pl.CostEstimate(
            flops=2 * 192 * 2560 * 512, bytes_accessed=3_600_000, transcendentals=0
        ),
        name="adapter",
    )(info, *pieces, wa, wb)


def normalize(gain_ref, rows, xs, out):
    tile = 96

    def step(i, _):
        at = pl.ds(pl.multiple_of(i * tile, 16), tile)
        values = xs[at, :].astype(F32)
        scale = lax.rsqrt(jnp.mean(values * values, axis=1, keepdims=True) + 1e-05)
        out[at, :] = (values * scale * gain_ref[...]).astype(BF)
        return 0

    lax.fori_loop(0, rows // tile, step, 0)


def gated(gate, up, at, x):
    g = lax.dot_general(gate[at, :], x[...], NT, preferred_element_type=F32)
    u = lax.dot_general(up[at, :], x[...], NT, preferred_element_type=F32)
    return (g * (1.0 / (1.0 + jnp.exp(-g))) * u).astype(BF)


def text_norm_kernel(info, gain_ref, *refs):
    own, other = refs[:8], refs[8:16]
    out_ref, xs, sem = refs[16:]
    z, s = info[0], info[1]
    rows = []
    for d in range(8):
        peer = lax.rem(z + d, 8)
        for part, ref in ((s, own[d]), (1 - s, other[d])):
            cols = pl.multiple_of((part * 8 + peer) * KPART, KPART)
            rows.append(
                pltpu.make_async_copy(
                    ref.at[pl.ds(0, TEXT)], xs.at[:, pl.ds(cols, KPART)], sem
                )
            )
    for copy in rows:
        copy.start()
    for copy in rows:
        copy.wait()
    normalize(gain_ref, TEXT, xs, out_ref)


def text_norm(info, gain, own, other):
    return pl.pallas_call(
        text_norm_kernel,
        out_shape=jax.ShapeDtypeStruct((TEXT, D), BF),
        in_specs=[smem(), vmem()] + [anywhere()] * 16,
        out_specs=vmem(),
        scratch_shapes=[pltpu.VMEM((TEXT, D), BF), pltpu.SemaphoreType.DMA],
        compiler_params=pltpu.CompilerParams(vmem_limit_bytes=18 * MIB),
        cost_estimate=pl.CostEstimate(
            flops=10 * TEXT * D, bytes_accessed=10_000_000, transcendentals=0
        ),
        name="text_norm",
    )(info, gain, *own, *other)


def place_kernel(all_ref, gate, up, sem):
    copies = []
    for chunk in range(N_DP):
        cols = slice(chunk * KPART, (chunk + 1) * KPART)
        for i, ref in enumerate((gate, up)):
            copies.append(pltpu.make_async_copy(all_ref.at[chunk, i], ref.at[:, cols], sem))
    for copy in copies:
        copy.start()
    for copy in copies:
        copy.wait()


def place_weights(gathered):
    return pl.pallas_call(
        place_kernel,
        out_shape=[jax.ShapeDtypeStruct((FPART, D), BF)] * 2,
        in_specs=[hbm()],
        out_specs=[vmem()] * 2,
        scratch_shapes=[pltpu.SemaphoreType.DMA],
        compiler_params=pltpu.CompilerParams(vmem_limit_bytes=44 * MIB),
        cost_estimate=pl.CostEstimate(flops=0, bytes_accessed=22_000_000, transcendentals=0),
        name="place_weights",
    )(gathered)


def text_tile_kernel(at, info, gate_ref, up_ref, x_ref, out_ref):
    dp = info[2]
    row = lax.broadcasted_iota(jnp.int32, (1, L_DEV), 1)
    compact = jnp.full((1, L_DEV), -1, jnp.int32)
    for k in range(4):
        u = dp * 4 + k
        first = info[OFFSET_AT + u] - dp * L_DEV
        end = first + info[ROWS_AT + u]
        shift = k * (REGION - TEXT_REGION)
        region = (row >= k * REGION) & (row < (k + 1) * REGION)
        compact = jnp.where(region & (row < first), row - shift, compact)
        compact = jnp.where(region & (row >= end), row - shift - info[ROWS_AT + u], compact)
    place = (lax.broadcasted_iota(jnp.int32, (TEXT, L_DEV), 0) == compact).astype(BF)
    hidden = gated(gate_ref, up_ref, pl.ds(*at), x_ref)
    out_ref[...] = jnp.dot(hidden, place, preferred_element_type=F32).astype(BF)


def text_tile(at, info, gate, up, x):
    return pl.pallas_call(
        functools.partial(text_tile_kernel, at),
        out_shape=jax.ShapeDtypeStruct((at[1], L_DEV), BF),
        in_specs=[smem()] + [vmem()] * 3,
        out_specs=vmem(),
        compiler_params=pltpu.CompilerParams(vmem_limit_bytes=24 * MIB),
        cost_estimate=pl.CostEstimate(
            flops=4 * TEXT * D * at[1], bytes_accessed=10_000_000, transcendentals=0
        ),
        name="text_tile",
    )(info, gate, up, x)


TILES = ((0, 256), (256, 256), (512, 176))


def speech_rows(info, gain_ref, pieces, xs, sem):
    copies = []
    for d in range(8):
        peer = lax.rem(info[0] + d, 8)
        for half in range(2):
            cols = pl.multiple_of((half * 8 + peer) * KPART, KPART)
            copies.append(
                pltpu.make_async_copy(
                    pieces[d].at[:, pl.ds(half * KPART, KPART)], xs.at[:, pl.ds(cols, KPART)], sem
                )
            )
    for copy in copies:
        copy.start()
    for copy in copies:
        copy.wait()
    normalize(gain_ref, ROWS, xs, xs)


def own_kernel(info, gain_ref, *refs):
    pieces, gate, up, out_ref, xs, sem = refs[:8], *refs[8:]
    speech_rows(info, gain_ref, pieces, xs, sem)
    for tile in TILES:
        at = pl.ds(*tile)
        out_ref[at, :] = gated(gate, up, at, xs)


def own_hidden(info, gain, pieces, gate, up):
    return pl.pallas_call(
        own_kernel,
        out_shape=jax.ShapeDtypeStruct((FPART, ROWS), BF),
        in_specs=[smem(), vmem()] + [anywhere()] * 8 + [vmem()] * 2,
        out_specs=vmem(),
        scratch_shapes=[pltpu.VMEM((ROWS, D), BF), pltpu.SemaphoreType.DMA],
        compiler_params=pltpu.CompilerParams(vmem_limit_bytes=24 * MIB),
        cost_estimate=pl.CostEstimate(
            flops=2 * ROWS * D * 2 * FPART, bytes_accessed=14_000_000, transcendentals=0
        ),
        name="own_hidden",
    )(info, gain, *pieces, gate, up)


def speech_kernel(info, gain_ref, *refs):
    pieces, gate, up, own_ref, texts = refs[:8], refs[8], refs[9], refs[10], refs[11:14]
    out_ref, xs, sem = refs[14:]
    s, dp = info[1], info[2]
    speech_rows(info, gain_ref, pieces, xs, sem)
    row = lax.broadcasted_iota(jnp.int32, (1, L_DEV), 1)
    sources = []
    for part in (s, 1 - s):
        source = jnp.full((1, L_DEV), -1, jnp.int32)
        for slot in range(2):
            u = dp * 4 + part * 2 + slot
            first = info[OFFSET_AT + u] - dp * L_DEV
            inside = (row >= first) & (row < first + info[ROWS_AT + u])
            source = jnp.where(inside, row - first + slot * MAXROWS, source)
        sources.append(source)
    slot_row = lax.broadcasted_iota(jnp.int32, (ROWS, L_DEV), 0)
    picks = [(slot_row == source).astype(BF) for source in sources]
    speech = (sources[0] >= 0) | (sources[1] >= 0)
    for (start, size), text_ref in zip(TILES, texts):
        at = pl.ds(start, size)
        placed = jnp.dot(own_ref[at, :], picks[0], preferred_element_type=F32) + jnp.dot(
            gated(gate, up, at, xs), picks[1], preferred_element_type=F32
        )
        out_ref[at, :] = jnp.where(speech, placed.astype(BF), text_ref[...])


def speech_hidden(info, gain, pieces, gate, up, own, texts):
    return pl.pallas_call(
        speech_kernel,
        out_shape=jax.ShapeDtypeStruct((FPART, L_DEV), BF),
        in_specs=[smem(), vmem()] + [anywhere()] * 8 + [vmem()] * 6,
        out_specs=vmem(),
        scratch_shapes=[pltpu.VMEM((ROWS, D), BF), pltpu.SemaphoreType.DMA],
        compiler_params=pltpu.CompilerParams(vmem_limit_bytes=24 * MIB),
        cost_estimate=pl.CostEstimate(
            flops=2 * ROWS * D * 2 * FPART, bytes_accessed=16_000_000, transcendentals=0
        ),
        name="speech_hidden",
    )(info, gain, *pieces, gate, up, own, *texts)


def per_device(
    mel_frames,
    utt_rows,
    utt_owner,
    utt_offset,
    conv1_w,
    conv2_w,
    adapter_w,
    text_rows,
    norm_gain,
    gate_w,
    up_w,
):
    s = lax.axis_index("section")
    place = [lax.axis_index("mp"), s, lax.axis_index("dp")]
    info = jnp.concatenate(
        [jnp.stack(place + [0] * 5).astype(jnp.int32), utt_rows, utt_owner, utt_offset]
    )
    gathered = lax.all_gather(jnp.stack([gate_w.T, up_w.T]), "dp", axis=0)

    def stage(values, *others):
        return lax.optimization_barrier((*values, *others))[: len(values)]

    def hop(forth, back):
        return shift_z(forth, 1), shift_z(back, 7)

    def last_hop(forth, back):
        half = forth.shape[0] // 2
        return jnp.concatenate(hop(forth[:half], back[half:]), 0)

    def by_offset(a, hops, last):
        return [a, hops[0][1], hops[1][1], hops[2][1], last, hops[2][0], hops[1][0], hops[0][0]]

    w1 = conv1_w.T
    w1_other = swap(w1)

    sent = pack(info, mel_frames.reshape(P_DEV, 4 * MELS))
    received = lax.all_to_all(sent, "dp", 0, 0, tiled=True)
    load = load_rows(info, *stage((text_rows, w1, w1_other), sent))

    t1 = hop(load, load)
    w2, wa = stage((conv2_w.T, adapter_w), load)
    w2_other, wa_other = swap(w2), swap(wa)
    t2 = hop(*stage(t1, sent, w2_other, wa_other))
    load_other, *o1 = [swap(v) for v in stage((load, *t1), *t2)]
    t3 = hop(*t2)
    o2 = [swap(v) for v in stage(t2, load_other, *o1, *t3)]
    forth, back = stage(t3, received, *o1)
    t4 = step_z(jnp.where(s == 0, forth, back))
    received_other = swap(received)
    maps = encoder(
        info, received, received_other, *by_offset(load, (t1, t2, t3), t4), w2, w2_other
    )

    m1 = hop(*stage((maps, maps), *o2))
    o3 = [swap(v) for v in stage((*t3, t4), maps)]
    m2 = hop(*m1)
    gain = norm_gain.reshape(1, D)
    text = stage(by_offset(load, (t1, t2, t3), t4), *m1)
    normed = text_norm(info, gain, text, by_offset(load_other, (o1, o2, o3), o3[2]))
    m3 = hop(*stage(m2, normed))
    m4 = last_hop(*m3)
    speech = adapter(info, by_offset(maps, (m1, m2, m3), m4), adapter_w, wa_other)

    s1 = hop(speech, speech)
    o0 = swap(speech)
    (here,) = stage((gathered,), speech)
    weights = place_weights(here)
    s2 = hop(*stage(s1, *weights))
    o1 = [swap(v) for v in stage(s1, o0, *weights)]
    texts = [text_tile(TILES[0], info, *weights, stage((normed,), *s1)[0])]
    s3 = hop(*stage(s2, *o1, *texts))
    o2 = [swap(v) for v in stage(s2, *o1, *texts)]
    texts.append(text_tile(TILES[1], info, *weights, stage((normed,), *s2)[0]))
    s4 = last_hop(*stage(s3, *o2, *texts))
    o3 = [swap(v) for v in stage(s3, *o2, *texts)]
    texts.append(text_tile(TILES[2], info, *weights, stage((normed,), *s3)[0]))
    (end,) = stage((s4,), *o3, *texts)
    o4 = swap(end)
    own = own_hidden(info, gain, by_offset(speech, (s1, s2, s3), end), *weights)
    other = by_offset(o0, (o1, o2, o3), o4)
    return speech_hidden(info, gain, other, *weights, own, texts).T


def solution(mesh):
    cols = ("section", "mp")
    return jax.shard_map(
        per_device,
        mesh=mesh,
        in_specs=(
            P("dp", None),
            P(),
            P(),
            P(),
            P(None, cols),
            P(None, cols),
            P(None, cols),
            P("dp", cols),
            P(),
            P("dp", cols),
            P("dp", cols),
        ),
        out_specs=P("dp", cols),
        check_vma=False,
    )
```

```python
import functools

import jax
import jax.numpy as jnp
from jax import lax
from jax.experimental import pallas as pl
from jax.experimental.pallas import tpu as pltpu
from jax.sharding import PartitionSpec as P

MELS = 128
C = 1280
D = 4096
N_DP = 16
MAXROWS = 96
ROWS = 2 * MAXROWS
P_DEV = 384
L_DEV = 768
HALF = MAXROWS // 2
TEXT_REGION = 144
TEXT = 4 * TEXT_REGION
REGION = 192
CPART = 80
FPART = 688
KPART = 256
BF = jnp.bfloat16
F32 = jnp.float32
MIB = 1024 * 1024
NT = (((1,), (1,)), ((), ()))


def step_z(a, k=1):
    return lax.ppermute(
        a,
        ("section", "mp"),
        [(c * 8 + z, c * 8 + (z + (k, 8 - k)[c]) % 8) for c in range(2) for z in range(8)],
    )


def shift_z(a, step):
    return lax.ppermute(a, "mp", [(i, (i + step) % 8) for i in range(8)])


def swap(a):
    return lax.ppermute(a, "section", [(0, 1), (1, 0)])


def gelu(v):
    return 0.5 * v * (1.0 + lax.erf(v * (0.5**0.5)))


def vmem():
    return pl.BlockSpec(memory_space=pltpu.VMEM)


def smem():
    return pl.BlockSpec(memory_space=pltpu.SMEM)


def anywhere():
    return pl.BlockSpec(memory_space=pl.ANY)


def hbm():
    return pl.BlockSpec(memory_space=pltpu.HBM)


ROWS_AT, OWNER_AT, OFFSET_AT = 8, 72, 136


def pack_kernel(info, quads_ref, out_ref, pick, first):
    s, dp = info[1], info[2]
    for b in range(N_DP):
        first[b] = P_DEV

    def look(b, start):
        for i in range(4):
            own = info[OWNER_AT + 4 * b + i] == dp
            first[b] = jnp.where(own, jnp.minimum(first[b], start), first[b])
            start += jnp.where(own, info[ROWS_AT + 4 * b + i], 0)
        return start

    lax.fori_loop(0, N_DP, look, jnp.int32(0))
    wanted = lax.broadcasted_iota(jnp.int32, (HALF, P_DEV), 0) + s * HALF
    held = lax.broadcasted_iota(jnp.int32, (HALF, P_DEV), 1)
    for b in range(N_DP):
        pick[b * HALF : (b + 1) * HALF, :] = (wanted + first[b] == held).astype(BF)
    out_ref[...] = jnp.dot(pick[...], quads_ref[...], preferred_element_type=F32).astype(BF)


def pack(info, quads):
    return pl.pallas_call(
        pack_kernel,
        out_shape=jax.ShapeDtypeStruct((N_DP * HALF, 4 * MELS), BF),
        in_specs=[smem(), vmem()],
        out_specs=vmem(),
        scratch_shapes=[
            pltpu.VMEM((N_DP * HALF, P_DEV), BF),
            pltpu.SMEM((N_DP,), jnp.int32),
        ],
        compiler_params=pltpu.CompilerParams(vmem_limit_bytes=16 * MIB),
        cost_estimate=pl.CostEstimate(
            flops=2 * 1536 * 384 * 512, bytes_accessed=2_000_000, transcendentals=0
        ),
        name="pack",
    )(info, quads)


def load_kernel(info, text_ref, w1_ref, w1_other_ref, out_ref):
    dp = info[2]
    compact = lax.broadcasted_iota(jnp.int32, (TEXT_REGION, REGION), 0)
    packed = lax.broadcasted_iota(jnp.int32, (TEXT_REGION, REGION), 1)
    for k in range(4):
        u = dp * 4 + k
        offset = info[OFFSET_AT + u] - u * REGION
        source = compact + jnp.where(compact >= offset, info[ROWS_AT + u], 0)
        out_ref[k * TEXT_REGION : (k + 1) * TEXT_REGION, :] = jnp.dot(
            (source == packed).astype(BF),
            text_ref[k * REGION : (k + 1) * REGION, :],
            preferred_element_type=F32,
        ).astype(BF)
    for i, ref in enumerate((w1_ref, w1_other_ref)):
        at = TEXT + i * CPART
        out_ref[at : at + CPART, :] = ref[:, : 2 * MELS]
        out_ref[TEXT + 2 * CPART :, i * MELS : (i + 1) * MELS] = ref[:, 2 * MELS :]


def load_rows(info, text, w1, w1_other):
    return pl.pallas_call(
        load_kernel,
        out_shape=jax.ShapeDtypeStruct((TEXT + 3 * CPART, KPART), BF),
        in_specs=[smem()] + [vmem()] * 3,
        out_specs=vmem(),
        compiler_params=pltpu.CompilerParams(vmem_limit_bytes=16 * MIB),
        cost_estimate=pl.CostEstimate(
            flops=2 * TEXT * REGION * KPART, bytes_accessed=1_000_000, transcendentals=0
        ),
        name="load_rows",
    )(info, text, w1, w1_other)


def encoder_kernel(info, received_ref, received_other_ref, *refs):
    loads, w2a_hbm, w2b_hbm = refs[:8], refs[8], refs[9]
    out_ref, w1, y, w2a_ref, w2b_ref, loaded, sems = refs[10:]
    sem = sems.at[0]
    rows_in = [
        pltpu.make_async_copy(loads[d].at[pl.ds(TEXT, 3 * CPART)], loaded.at[d], sems.at[1])
        for d in range(8)
    ]
    for copy in rows_in:
        copy.start()
    fetches = [
        pltpu.make_async_copy(w2a_hbm, w2a_ref, sem),
        pltpu.make_async_copy(w2b_hbm, w2b_ref, sem),
    ]
    for fetch in fetches:
        fetch.start()
    z, s, dp = info[0], info[1], info[2]

    for copy in rows_in:
        copy.wait()
    for d in range(8):
        peer = lax.rem(z + d, 8)
        for i in range(2):
            part = jnp.where(s == i, 0, 1)
            at = pl.ds(pl.multiple_of((part * 8 + peer) * CPART, 16), CPART)
            w1[at, : 2 * MELS] = loaded[d, i * CPART : (i + 1) * CPART, :]
            w1[at, 2 * MELS :] = loaded[d, 2 * CPART :, i * MELS : (i + 1) * MELS]

    row = lax.broadcasted_iota(jnp.int32, (ROWS, 1), 0)
    slot_row = jnp.where(row < MAXROWS, row, row - MAXROWS)
    source = jnp.full((ROWS, 1), -1, jnp.int32)
    part = jnp.zeros((ROWS, 1), jnp.int32)
    for slot in range(2):
        u = dp * 4 + s * 2 + slot
        owner = info[OWNER_AT + u]
        at = jnp.int32(0)
        for earlier in range(4):
            v = dp * 4 + earlier
            at += jnp.where((v < u) & (info[OWNER_AT + v] == owner), info[ROWS_AT + v], 0)
        here = (row >= slot * MAXROWS) & (row < (slot + 1) * MAXROWS) & (slot_row < info[ROWS_AT + u])
        late = at + slot_row >= HALF
        source = jnp.where(
            here, owner * HALF + at + slot_row - jnp.where(late, HALF, 0), source
        )
        part = jnp.where(here & late, 1, part)
    active = source >= 0
    every = lax.broadcasted_iota(jnp.int32, (ROWS, N_DP * HALF), 1)
    x = (
        jnp.dot(
            (jnp.where(part == s, source, -1) == every).astype(BF),
            received_ref[...],
            preferred_element_type=F32,
        )
        + jnp.dot(
            (jnp.where(part == s, -1, source) == every).astype(BF),
            received_other_ref[...],
            preferred_element_type=F32,
        )
    ).astype(BF)

    head = x[:, :MELS].astype(F32)
    tail = x[:, 3 * MELS :].astype(F32)
    before = jnp.where(slot_row == 0, 0.0, pltpu.roll(tail, 1, 0)).astype(BF)
    following = jnp.where(
        slot_row == MAXROWS - 1, 0.0, pltpu.roll(head, ROWS - 1, 0)
    ).astype(BF)
    wide = jnp.concatenate([before, x, following], 1)
    for tile in range(C // 256):
        weight = w1[tile * 256 : (tile + 1) * 256, :]
        for q in range(4):
            total = lax.dot_general(
                wide[:, q * MELS : (q + 3) * MELS], weight, NT, preferred_element_type=F32
            )
            y[q, :, tile * 256 : (tile + 1) * 256] = jnp.where(active, gelu(total), 0.0).astype(BF)
    last = y[3].astype(F32)
    y_before = jnp.where(slot_row == 0, 0.0, pltpu.roll(last, 1, 0)).astype(BF)
    dot = functools.partial(lax.dot_general, dimension_numbers=NT, preferred_element_type=F32)
    for fetch in fetches:
        fetch.wait()

    def second(ref):
        w_before, w_mid, w_after = ref[:, :C], ref[:, C : 2 * C], ref[:, 2 * C :]
        even = dot(y_before, w_before) + dot(y[0], w_mid) + dot(y[1], w_after)
        odd = dot(y[1], w_before) + dot(y[2], w_mid) + dot(y[3], w_after)
        return even, odd

    mine, others = second(w2a_ref), second(w2b_ref)
    parts = []
    for h in range(2):
        parts += [jnp.where(s == 0, mine[h], others[h]), jnp.where(s == 0, others[h], mine[h])]
    both = jnp.concatenate(parts, 1)
    out_ref[...] = jnp.where(active, gelu(both), 0.0).astype(BF)


def encoder(info, *arrays):
    return pl.pallas_call(
        encoder_kernel,
        out_shape=jax.ShapeDtypeStruct((ROWS, 4 * CPART), BF),
        in_specs=[smem(), vmem(), vmem()] + [anywhere()] * 8 + [hbm()] * 2,
        out_specs=vmem(),
        scratch_shapes=[
            pltpu.VMEM((C, 3 * MELS), BF),
            pltpu.VMEM((4, ROWS, C), BF),
            pltpu.VMEM((CPART, 3 * C), BF),
            pltpu.VMEM((CPART, 3 * C), BF),
            pltpu.VMEM((8, 3 * CPART, 2 * MELS), BF),
            pltpu.SemaphoreType.DMA((2,)),
        ],
        compiler_params=pltpu.CompilerParams(vmem_limit_bytes=24 * MIB),
        cost_estimate=pl.CostEstimate(
            flops=2 * 192 * 4 * (384 * C + 3840 * 80), bytes_accessed=5_000_000, transcendentals=0
        ),
        name="encoder",
    )(info, *arrays)


def adapter_kernel(info, *refs):
    pieces, wa_ref, wb_ref, out_ref = refs[:8], refs[8], refs[9], refs[10]
    z, s = info[0], info[1]
    totals = [jnp.zeros((ROWS, KPART), F32), jnp.zeros((ROWS, KPART), F32)]
    for d in range(8):
        piece = pieces[d][...]
        peer = lax.rem(z + d, 8)
        for i, ref in enumerate((wa_ref, wb_ref)):
            weight = jnp.concatenate(
                [ref[pl.ds(pl.multiple_of((8 * j + peer) * CPART, 16), CPART), :] for j in range(4)],
                0,
            )
            totals[i] += jnp.dot(piece, weight, preferred_element_type=F32)
    mine, others = totals
    out_ref[:, :KPART] = jnp.where(s == 0, mine, others).astype(BF)
    out_ref[:, KPART:] = jnp.where(s == 0, others, mine).astype(BF)


def adapter(info, pieces, wa, wb):
    return pl.pallas_call(
        adapter_kernel,
        out_shape=jax.ShapeDtypeStruct((ROWS, 2 * KPART), BF),
        in_specs=[smem()] + [vmem()] * 10,
        out_specs=vmem(),
        compiler_params=pltpu.CompilerParams(vmem_limit_bytes=24 * MIB),
        cost_estimate=pl.CostEstimate(
            flops=2 * 192 * 2560 * 512, bytes_accessed=3_600_000, transcendentals=0
        ),
        name="adapter",
    )(info, *pieces, wa, wb)


def normalize(gain_ref, rows, xs, out):
    tile = 96

    def step(i, _):
        at = pl.ds(pl.multiple_of(i * tile, 16), tile)
        values = xs[at, :].astype(F32)
        scale = lax.rsqrt(jnp.mean(values * values, axis=1, keepdims=True) + 1e-05)
        out[at, :] = (values * scale * gain_ref[...]).astype(BF)
        return 0

    lax.fori_loop(0, rows // tile, step, 0)


def gated(gate, up, at, x):
    g = lax.dot_general(gate[at, :], x[...], NT, preferred_element_type=F32)
    u = lax.dot_general(up[at, :], x[...], NT, preferred_element_type=F32)
    return (g * (1.0 / (1.0 + jnp.exp(-g))) * u).astype(BF)


def text_norm_kernel(info, gain_ref, *refs):
    own, other = refs[:8], refs[8:16]
    out_ref, xs, sem = refs[16:]
    z, s = info[0], info[1]
    rows = []
    for d in range(8):
        peer = lax.rem(z + d, 8)
        for part, ref in ((s, own[d]), (1 - s, other[d])):
            cols = pl.multiple_of((part * 8 + peer) * KPART, KPART)
            rows.append(
                pltpu.make_async_copy(
                    ref.at[pl.ds(0, TEXT)], xs.at[:, pl.ds(cols, KPART)], sem
                )
            )
    for copy in rows:
        copy.start()
    for copy in rows:
        copy.wait()
    normalize(gain_ref, TEXT, xs, out_ref)


def text_norm(info, gain, own, other):
    return pl.pallas_call(
        text_norm_kernel,
        out_shape=jax.ShapeDtypeStruct((TEXT, D), BF),
        in_specs=[smem(), vmem()] + [anywhere()] * 16,
        out_specs=vmem(),
        scratch_shapes=[pltpu.VMEM((TEXT, D), BF), pltpu.SemaphoreType.DMA],
        compiler_params=pltpu.CompilerParams(vmem_limit_bytes=18 * MIB),
        cost_estimate=pl.CostEstimate(
            flops=10 * TEXT * D, bytes_accessed=10_000_000, transcendentals=0
        ),
        name="text_norm",
    )(info, gain, *own, *other)


def place_kernel(all_ref, gate, up, sem):
    copies = []
    for chunk in range(N_DP):
        cols = slice(chunk * KPART, (chunk + 1) * KPART)
        for i, ref in enumerate((gate, up)):
            copies.append(pltpu.make_async_copy(all_ref.at[chunk, i], ref.at[:, cols], sem))
    for copy in copies:
        copy.start()
    for copy in copies:
        copy.wait()


def place_weights(gathered):
    return pl.pallas_call(
        place_kernel,
        out_shape=[jax.ShapeDtypeStruct((FPART, D), BF)] * 2,
        in_specs=[hbm()],
        out_specs=[vmem()] * 2,
        scratch_shapes=[pltpu.SemaphoreType.DMA],
        compiler_params=pltpu.CompilerParams(vmem_limit_bytes=38 * MIB),
        cost_estimate=pl.CostEstimate(flops=0, bytes_accessed=22_000_000, transcendentals=0),
        name="place_weights",
    )(gathered)


def text_tile_kernel(at, info, gate_ref, up_ref, x_ref, out_ref):
    dp = info[2]
    row = lax.broadcasted_iota(jnp.int32, (1, L_DEV), 1)
    compact = jnp.full((1, L_DEV), -1, jnp.int32)
    for k in range(4):
        u = dp * 4 + k
        first = info[OFFSET_AT + u] - dp * L_DEV
        end = first + info[ROWS_AT + u]
        shift = k * (REGION - TEXT_REGION)
        region = (row >= k * REGION) & (row < (k + 1) * REGION)
        compact = jnp.where(region & (row < first), row - shift, compact)
        compact = jnp.where(region & (row >= end), row - shift - info[ROWS_AT + u], compact)
    place = (lax.broadcasted_iota(jnp.int32, (TEXT, L_DEV), 0) == compact).astype(BF)
    hidden = gated(gate_ref, up_ref, pl.ds(*at), x_ref)
    out_ref[...] = jnp.dot(hidden, place, preferred_element_type=F32).astype(BF)


def text_tile(at, info, gate, up, x):
    return pl.pallas_call(
        functools.partial(text_tile_kernel, at),
        out_shape=jax.ShapeDtypeStruct((at[1], L_DEV), BF),
        in_specs=[smem()] + [vmem()] * 3,
        out_specs=vmem(),
        compiler_params=pltpu.CompilerParams(vmem_limit_bytes=24 * MIB),
        cost_estimate=pl.CostEstimate(
            flops=4 * TEXT * D * at[1], bytes_accessed=10_000_000, transcendentals=0
        ),
        name="text_tile",
    )(info, gate, up, x)


TILES = ((0, 256), (256, 256), (512, 176))


def speech_rows(info, gain_ref, pieces, xs, sem):
    copies = []
    for d in range(8):
        peer = lax.rem(info[0] + d, 8)
        for half in range(2):
            cols = pl.multiple_of((half * 8 + peer) * KPART, KPART)
            copies.append(
                pltpu.make_async_copy(
                    pieces[d].at[:, pl.ds(half * KPART, KPART)], xs.at[:, pl.ds(cols, KPART)], sem
                )
            )
    for copy in copies:
        copy.start()
    for copy in copies:
        copy.wait()
    normalize(gain_ref, ROWS, xs, xs)


def own_kernel(info, gain_ref, *refs):
    pieces, gate, up, out_ref, xs, sem = refs[:8], *refs[8:]
    speech_rows(info, gain_ref, pieces, xs, sem)
    for tile in TILES:
        at = pl.ds(*tile)
        out_ref[at, :] = gated(gate, up, at, xs)


def own_hidden(info, gain, pieces, gate, up):
    return pl.pallas_call(
        own_kernel,
        out_shape=jax.ShapeDtypeStruct((FPART, ROWS), BF),
        in_specs=[smem(), vmem()] + [anywhere()] * 8 + [vmem()] * 2,
        out_specs=vmem(),
        scratch_shapes=[pltpu.VMEM((ROWS, D), BF), pltpu.SemaphoreType.DMA],
        compiler_params=pltpu.CompilerParams(vmem_limit_bytes=24 * MIB),
        cost_estimate=pl.CostEstimate(
            flops=2 * ROWS * D * 2 * FPART, bytes_accessed=14_000_000, transcendentals=0
        ),
        name="own_hidden",
    )(info, gain, *pieces, gate, up)


def speech_kernel(info, gain_ref, *refs):
    pieces, gate, up, own_ref, texts = refs[:8], refs[8], refs[9], refs[10], refs[11:14]
    out_ref, xs, sem = refs[14:]
    s, dp = info[1], info[2]
    speech_rows(info, gain_ref, pieces, xs, sem)
    row = lax.broadcasted_iota(jnp.int32, (1, L_DEV), 1)
    sources = []
    for part in (s, 1 - s):
        source = jnp.full((1, L_DEV), -1, jnp.int32)
        for slot in range(2):
            u = dp * 4 + part * 2 + slot
            first = info[OFFSET_AT + u] - dp * L_DEV
            inside = (row >= first) & (row < first + info[ROWS_AT + u])
            source = jnp.where(inside, row - first + slot * MAXROWS, source)
        sources.append(source)
    slot_row = lax.broadcasted_iota(jnp.int32, (ROWS, L_DEV), 0)
    picks = [(slot_row == source).astype(BF) for source in sources]
    speech = (sources[0] >= 0) | (sources[1] >= 0)
    for (start, size), text_ref in zip(TILES, texts):
        at = pl.ds(start, size)
        placed = jnp.dot(own_ref[at, :], picks[0], preferred_element_type=F32) + jnp.dot(
            gated(gate, up, at, xs), picks[1], preferred_element_type=F32
        )
        out_ref[at, :] = jnp.where(speech, placed.astype(BF), text_ref[...])


def speech_hidden(info, gain, pieces, gate, up, own, texts):
    return pl.pallas_call(
        speech_kernel,
        out_shape=jax.ShapeDtypeStruct((FPART, L_DEV), BF),
        in_specs=[smem(), vmem()] + [anywhere()] * 8 + [vmem()] * 6,
        out_specs=vmem(),
        scratch_shapes=[pltpu.VMEM((ROWS, D), BF), pltpu.SemaphoreType.DMA],
        compiler_params=pltpu.CompilerParams(vmem_limit_bytes=24 * MIB),
        cost_estimate=pl.CostEstimate(
            flops=2 * ROWS * D * 2 * FPART, bytes_accessed=16_000_000, transcendentals=0
        ),
        name="speech_hidden",
    )(info, gain, *pieces, gate, up, own, *texts)


def per_device(
    mel_frames,
    utt_rows,
    utt_owner,
    utt_offset,
    conv1_w,
    conv2_w,
    adapter_w,
    text_rows,
    norm_gain,
    gate_w,
    up_w,
):
    s = lax.axis_index("section")
    place = [lax.axis_index("mp"), s, lax.axis_index("dp")]
    info = jnp.concatenate(
        [jnp.stack(place + [0] * 5).astype(jnp.int32), utt_rows, utt_owner, utt_offset]
    )
    def stage(values, *others):
        return lax.optimization_barrier((*values, *others))[: len(values)]

    def hop(forth, back):
        return shift_z(forth, 1), shift_z(back, 7)

    def last_hop(forth, back):
        half = forth.shape[0] // 2
        return jnp.concatenate(hop(forth[:half], back[half:]), 0)

    def by_offset(a, hops, last):
        return [a, hops[0][1], hops[1][1], hops[2][1], last, hops[2][0], hops[1][0], hops[0][0]]

    w1 = conv1_w.T
    w1_other = swap(w1)

    sent = pack(info, mel_frames.reshape(P_DEV, 4 * MELS))
    received = lax.all_to_all(sent, "dp", 0, 0, tiled=True)
    load = load_rows(info, *stage((text_rows, w1, w1_other), sent))

    gathered = lax.all_gather(jnp.stack(stage((gate_w.T, up_w.T), load)), "dp", axis=0)

    t1 = hop(load, load)
    w2, wa = stage((conv2_w.T, adapter_w), load)
    w2_other, wa_other = swap(w2), swap(wa)
    t2 = hop(*stage(t1, sent, w2_other, wa_other))
    load_other, *o1 = [swap(v) for v in stage((load, *t1), *t2)]
    t3 = hop(*t2)
    o2 = [swap(v) for v in stage(t2, load_other, *o1, *t3)]
    forth, back = stage(t3, received, *o1)
    t4 = step_z(jnp.where(s == 0, forth, back))
    received_other = swap(received)
    maps = encoder(
        info, received, received_other, *by_offset(load, (t1, t2, t3), t4), w2, w2_other
    )

    m1 = hop(*stage((maps, maps), *o2))
    o3 = [swap(v) for v in stage((*t3, t4), maps)]
    m2 = hop(*m1)
    gain = norm_gain.reshape(1, D)
    text = stage(by_offset(load, (t1, t2, t3), t4), *m1)
    normed = text_norm(info, gain, text, by_offset(load_other, (o1, o2, o3), o3[2]))
    m3 = hop(*stage(m2, normed))
    m4 = last_hop(*m3)
    speech = adapter(info, by_offset(maps, (m1, m2, m3), m4), adapter_w, wa_other)

    s1 = hop(speech, speech)
    (here,) = stage((gathered,), speech)
    weights = place_weights(here)
    o0 = swap(*stage((speech,), *weights))
    s2 = hop(*s1)
    o1 = [swap(v) for v in stage(s1, o0)]
    texts = [text_tile(TILES[0], info, *weights, stage((normed,), *s1)[0])]
    s3 = hop(*stage(s2, *o1, *texts))
    o2 = [swap(v) for v in stage(s2, *o1, *texts)]
    texts.append(text_tile(TILES[1], info, *weights, stage((normed,), *s2)[0]))
    s4 = last_hop(*stage(s3, *o2, *texts))
    o3 = [swap(v) for v in stage(s3, *o2, *texts)]
    texts.append(text_tile(TILES[2], info, *weights, stage((normed,), *s3)[0]))
    (end,) = stage((s4,), *o3, *texts)
    o4 = swap(end)
    own = own_hidden(info, gain, by_offset(speech, (s1, s2, s3), end), *weights)
    other = by_offset(o0, (o1, o2, o3), o4)
    return speech_hidden(info, gain, other, *weights, own, texts).T


def solution(mesh):
    cols = ("section", "mp")
    return jax.shard_map(
        per_device,
        mesh=mesh,
        in_specs=(
            P("dp", None),
            P(),
            P(),
            P(),
            P(None, cols),
            P(None, cols),
            P(None, cols),
            P("dp", cols),
            P(),
            P("dp", cols),
            P("dp", cols),
        ),
        out_specs=P("dp", cols),
        check_vma=False,
    )
```

```python
import functools

import jax
import jax.numpy as jnp
from jax import lax
from jax.experimental import pallas as pl
from jax.experimental.pallas import tpu as pltpu
from jax.sharding import PartitionSpec as P

MELS = 128
C = 1280
D = 4096
N_DP = 16
MAXROWS = 96
ROWS = 2 * MAXROWS
P_DEV = 384
L_DEV = 768
HALF = MAXROWS // 2
TEXT_REGION = 144
TEXT = 4 * TEXT_REGION
REGION = 192
CPART = 80
FPART = 688
KPART = 256
BF = jnp.bfloat16
F32 = jnp.float32
MIB = 1024 * 1024
NT = (((1,), (1,)), ((), ()))


def step_z(a, k=1):
    return lax.ppermute(
        a,
        ("section", "mp"),
        [(c * 8 + z, c * 8 + (z + (k, 8 - k)[c]) % 8) for c in range(2) for z in range(8)],
    )


def shift_z(a, step):
    return lax.ppermute(a, "mp", [(i, (i + step) % 8) for i in range(8)])


def swap(a):
    return lax.ppermute(a, "section", [(0, 1), (1, 0)])


def gelu(v):
    return 0.5 * v * (1.0 + lax.erf(v * (0.5**0.5)))


def vmem():
    return pl.BlockSpec(memory_space=pltpu.VMEM)


def smem():
    return pl.BlockSpec(memory_space=pltpu.SMEM)


def anywhere():
    return pl.BlockSpec(memory_space=pl.ANY)


def hbm():
    return pl.BlockSpec(memory_space=pltpu.HBM)


ROWS_AT, OWNER_AT, OFFSET_AT = 8, 72, 136


def pack_kernel(info, quads_ref, out_ref, pick, first):
    s, dp = info[1], info[2]
    for b in range(N_DP):
        first[b] = P_DEV

    def look(b, start):
        for i in range(4):
            own = info[OWNER_AT + 4 * b + i] == dp
            first[b] = jnp.where(own, jnp.minimum(first[b], start), first[b])
            start += jnp.where(own, info[ROWS_AT + 4 * b + i], 0)
        return start

    lax.fori_loop(0, N_DP, look, jnp.int32(0))
    wanted = lax.broadcasted_iota(jnp.int32, (HALF, P_DEV), 0) + s * HALF
    held = lax.broadcasted_iota(jnp.int32, (HALF, P_DEV), 1)
    for b in range(N_DP):
        pick[b * HALF : (b + 1) * HALF, :] = (wanted + first[b] == held).astype(BF)
    out_ref[...] = jnp.dot(pick[...], quads_ref[...], preferred_element_type=F32).astype(BF)


def pack(info, quads):
    return pl.pallas_call(
        pack_kernel,
        out_shape=jax.ShapeDtypeStruct((N_DP * HALF, 4 * MELS), BF),
        in_specs=[smem(), vmem()],
        out_specs=vmem(),
        scratch_shapes=[
            pltpu.VMEM((N_DP * HALF, P_DEV), BF),
            pltpu.SMEM((N_DP,), jnp.int32),
        ],
        compiler_params=pltpu.CompilerParams(vmem_limit_bytes=16 * MIB),
        cost_estimate=pl.CostEstimate(
            flops=2 * 1536 * 384 * 512, bytes_accessed=2_000_000, transcendentals=0
        ),
        name="pack",
    )(info, quads)


def load_kernel(info, text_ref, w1_ref, w1_other_ref, out_ref):
    dp = info[2]
    compact = lax.broadcasted_iota(jnp.int32, (TEXT_REGION, REGION), 0)
    packed = lax.broadcasted_iota(jnp.int32, (TEXT_REGION, REGION), 1)
    for k in range(4):
        u = dp * 4 + k
        offset = info[OFFSET_AT + u] - u * REGION
        source = compact + jnp.where(compact >= offset, info[ROWS_AT + u], 0)
        out_ref[k * TEXT_REGION : (k + 1) * TEXT_REGION, :] = jnp.dot(
            (source == packed).astype(BF),
            text_ref[k * REGION : (k + 1) * REGION, :],
            preferred_element_type=F32,
        ).astype(BF)
    for i, ref in enumerate((w1_ref, w1_other_ref)):
        at = TEXT + i * CPART
        out_ref[at : at + CPART, :] = ref[:, : 2 * MELS]
        out_ref[TEXT + 2 * CPART :, i * MELS : (i + 1) * MELS] = ref[:, 2 * MELS :]


def load_rows(info, text, w1, w1_other):
    return pl.pallas_call(
        load_kernel,
        out_shape=jax.ShapeDtypeStruct((TEXT + 3 * CPART, KPART), BF),
        in_specs=[smem()] + [vmem()] * 3,
        out_specs=vmem(),
        compiler_params=pltpu.CompilerParams(vmem_limit_bytes=16 * MIB),
        cost_estimate=pl.CostEstimate(
            flops=2 * TEXT * REGION * KPART, bytes_accessed=1_000_000, transcendentals=0
        ),
        name="load_rows",
    )(info, text, w1, w1_other)


def encoder_kernel(info, received_ref, received_other_ref, *refs):
    loads, w2a_hbm, w2b_hbm = refs[:8], refs[8], refs[9]
    out_ref, w1, y, w2a_ref, w2b_ref, loaded, sems = refs[10:]
    sem = sems.at[0]
    rows_in = [
        pltpu.make_async_copy(loads[d].at[pl.ds(TEXT, 3 * CPART)], loaded.at[d], sems.at[1])
        for d in range(8)
    ]
    for copy in rows_in:
        copy.start()
    fetches = [
        pltpu.make_async_copy(w2a_hbm, w2a_ref, sem),
        pltpu.make_async_copy(w2b_hbm, w2b_ref, sem),
    ]
    for fetch in fetches:
        fetch.start()
    z, s, dp = info[0], info[1], info[2]

    for copy in rows_in:
        copy.wait()
    for d in range(8):
        peer = lax.rem(z + d, 8)
        for i in range(2):
            part = jnp.where(s == i, 0, 1)
            at = pl.ds(pl.multiple_of((part * 8 + peer) * CPART, 16), CPART)
            w1[at, : 2 * MELS] = loaded[d, i * CPART : (i + 1) * CPART, :]
            w1[at, 2 * MELS :] = loaded[d, 2 * CPART :, i * MELS : (i + 1) * MELS]

    row = lax.broadcasted_iota(jnp.int32, (ROWS, 1), 0)
    slot_row = jnp.where(row < MAXROWS, row, row - MAXROWS)
    source = jnp.full((ROWS, 1), -1, jnp.int32)
    part = jnp.zeros((ROWS, 1), jnp.int32)
    for slot in range(2):
        u = dp * 4 + s * 2 + slot
        owner = info[OWNER_AT + u]
        at = jnp.int32(0)
        for earlier in range(4):
            v = dp * 4 + earlier
            at += jnp.where((v < u) & (info[OWNER_AT + v] == owner), info[ROWS_AT + v], 0)
        here = (row >= slot * MAXROWS) & (row < (slot + 1) * MAXROWS) & (slot_row < info[ROWS_AT + u])
        late = at + slot_row >= HALF
        source = jnp.where(
            here, owner * HALF + at + slot_row - jnp.where(late, HALF, 0), source
        )
        part = jnp.where(here & late, 1, part)
    active = source >= 0
    every = lax.broadcasted_iota(jnp.int32, (ROWS, N_DP * HALF), 1)
    x = (
        jnp.dot(
            (jnp.where(part == s, source, -1) == every).astype(BF),
            received_ref[...],
            preferred_element_type=F32,
        )
        + jnp.dot(
            (jnp.where(part == s, -1, source) == every).astype(BF),
            received_other_ref[...],
            preferred_element_type=F32,
        )
    ).astype(BF)

    head = x[:, :MELS].astype(F32)
    tail = x[:, 3 * MELS :].astype(F32)
    before = jnp.where(slot_row == 0, 0.0, pltpu.roll(tail, 1, 0)).astype(BF)
    following = jnp.where(
        slot_row == MAXROWS - 1, 0.0, pltpu.roll(head, ROWS - 1, 0)
    ).astype(BF)
    wide = jnp.concatenate([before, x, following], 1)
    for tile in range(C // 256):
        weight = w1[tile * 256 : (tile + 1) * 256, :]
        for q in range(4):
            total = lax.dot_general(
                wide[:, q * MELS : (q + 3) * MELS], weight, NT, preferred_element_type=F32
            )
            y[q, :, tile * 256 : (tile + 1) * 256] = jnp.where(active, gelu(total), 0.0).astype(BF)
    last = y[3].astype(F32)
    y_before = jnp.where(slot_row == 0, 0.0, pltpu.roll(last, 1, 0)).astype(BF)
    dot = functools.partial(lax.dot_general, dimension_numbers=NT, preferred_element_type=F32)
    for fetch in fetches:
        fetch.wait()

    def second(ref):
        w_before, w_mid, w_after = ref[:, :C], ref[:, C : 2 * C], ref[:, 2 * C :]
        even = dot(y_before, w_before) + dot(y[0], w_mid) + dot(y[1], w_after)
        odd = dot(y[1], w_before) + dot(y[2], w_mid) + dot(y[3], w_after)
        return even, odd

    mine, others = second(w2a_ref), second(w2b_ref)
    parts = []
    for h in range(2):
        parts += [jnp.where(s == 0, mine[h], others[h]), jnp.where(s == 0, others[h], mine[h])]
    both = jnp.concatenate(parts, 1)
    out_ref[...] = jnp.where(active, gelu(both), 0.0).astype(BF)


def encoder(info, *arrays):
    return pl.pallas_call(
        encoder_kernel,
        out_shape=jax.ShapeDtypeStruct((ROWS, 4 * CPART), BF),
        in_specs=[smem(), vmem(), vmem()] + [anywhere()] * 8 + [hbm()] * 2,
        out_specs=vmem(),
        scratch_shapes=[
            pltpu.VMEM((C, 3 * MELS), BF),
            pltpu.VMEM((4, ROWS, C), BF),
            pltpu.VMEM((CPART, 3 * C), BF),
            pltpu.VMEM((CPART, 3 * C), BF),
            pltpu.VMEM((8, 3 * CPART, 2 * MELS), BF),
            pltpu.SemaphoreType.DMA((2,)),
        ],
        compiler_params=pltpu.CompilerParams(vmem_limit_bytes=24 * MIB),
        cost_estimate=pl.CostEstimate(
            flops=2 * 192 * 4 * (384 * C + 3840 * 80), bytes_accessed=5_000_000, transcendentals=0
        ),
        name="encoder",
    )(info, *arrays)


def adapter_kernel(info, *refs):
    pieces, wa_ref, wb_ref, out_ref = refs[:8], refs[8], refs[9], refs[10]
    z, s = info[0], info[1]
    totals = [jnp.zeros((ROWS, KPART), F32), jnp.zeros((ROWS, KPART), F32)]
    for d in range(8):
        piece = pieces[d][...]
        peer = lax.rem(z + d, 8)
        for i, ref in enumerate((wa_ref, wb_ref)):
            weight = jnp.concatenate(
                [ref[pl.ds(pl.multiple_of((8 * j + peer) * CPART, 16), CPART), :] for j in range(4)],
                0,
            )
            totals[i] += jnp.dot(piece, weight, preferred_element_type=F32)
    mine, others = totals
    out_ref[:, :KPART] = jnp.where(s == 0, mine, others).astype(BF)
    out_ref[:, KPART:] = jnp.where(s == 0, others, mine).astype(BF)


def adapter(info, pieces, wa, wb):
    return pl.pallas_call(
        adapter_kernel,
        out_shape=jax.ShapeDtypeStruct((ROWS, 2 * KPART), BF),
        in_specs=[smem()] + [vmem()] * 10,
        out_specs=vmem(),
        compiler_params=pltpu.CompilerParams(vmem_limit_bytes=24 * MIB),
        cost_estimate=pl.CostEstimate(
            flops=2 * 192 * 2560 * 512, bytes_accessed=3_600_000, transcendentals=0
        ),
        name="adapter",
    )(info, *pieces, wa, wb)


def normalize(gain_ref, rows, xs, out):
    tile = 96

    def step(i, _):
        at = pl.ds(pl.multiple_of(i * tile, 16), tile)
        values = xs[at, :].astype(F32)
        scale = lax.rsqrt(jnp.mean(values * values, axis=1, keepdims=True) + 1e-05)
        out[at, :] = (values * scale * gain_ref[...]).astype(BF)
        return 0

    lax.fori_loop(0, rows // tile, step, 0)


def gated(gate, up, at, x):
    g = lax.dot_general(gate[at, :], x[...], NT, preferred_element_type=F32)
    u = lax.dot_general(up[at, :], x[...], NT, preferred_element_type=F32)
    return (g * (1.0 / (1.0 + jnp.exp(-g))) * u).astype(BF)


def text_norm_kernel(info, gain_ref, *refs):
    own, other = refs[:8], refs[8:16]
    out_ref, xs, sem = refs[16:]
    z, s = info[0], info[1]
    rows = []
    for d in range(8):
        peer = lax.rem(z + d, 8)
        for part, ref in ((s, own[d]), (1 - s, other[d])):
            cols = pl.multiple_of((part * 8 + peer) * KPART, KPART)
            rows.append(
                pltpu.make_async_copy(
                    ref.at[pl.ds(0, TEXT)], xs.at[:, pl.ds(cols, KPART)], sem
                )
            )
    for copy in rows:
        copy.start()
    for copy in rows:
        copy.wait()
    normalize(gain_ref, TEXT, xs, out_ref)


def text_norm(info, gain, own, other):
    return pl.pallas_call(
        text_norm_kernel,
        out_shape=jax.ShapeDtypeStruct((TEXT, D), BF),
        in_specs=[smem(), vmem()] + [anywhere()] * 16,
        out_specs=vmem(),
        scratch_shapes=[pltpu.VMEM((TEXT, D), BF), pltpu.SemaphoreType.DMA],
        compiler_params=pltpu.CompilerParams(vmem_limit_bytes=18 * MIB),
        cost_estimate=pl.CostEstimate(
            flops=10 * TEXT * D, bytes_accessed=10_000_000, transcendentals=0
        ),
        name="text_norm",
    )(info, gain, *own, *other)


def place_kernel(all_ref, gate, up, sem):
    copies = []
    for chunk in range(N_DP):
        cols = slice(chunk * KPART, (chunk + 1) * KPART)
        for i, ref in enumerate((gate, up)):
            copies.append(pltpu.make_async_copy(all_ref.at[chunk, i], ref.at[:, cols], sem))
    for copy in copies:
        copy.start()
    for copy in copies:
        copy.wait()


def place_weights(gathered):
    return pl.pallas_call(
        place_kernel,
        out_shape=[jax.ShapeDtypeStruct((FPART, D), BF)] * 2,
        in_specs=[hbm()],
        out_specs=[vmem()] * 2,
        scratch_shapes=[pltpu.SemaphoreType.DMA],
        compiler_params=pltpu.CompilerParams(vmem_limit_bytes=38 * MIB),
        cost_estimate=pl.CostEstimate(flops=0, bytes_accessed=22_000_000, transcendentals=0),
        name="place_weights",
    )(gathered)


def text_tile_kernel(at, info, gate_ref, up_ref, x_ref, out_ref):
    dp = info[2]
    row = lax.broadcasted_iota(jnp.int32, (1, L_DEV), 1)
    compact = jnp.full((1, L_DEV), -1, jnp.int32)
    for k in range(4):
        u = dp * 4 + k
        first = info[OFFSET_AT + u] - dp * L_DEV
        end = first + info[ROWS_AT + u]
        shift = k * (REGION - TEXT_REGION)
        region = (row >= k * REGION) & (row < (k + 1) * REGION)
        compact = jnp.where(region & (row < first), row - shift, compact)
        compact = jnp.where(region & (row >= end), row - shift - info[ROWS_AT + u], compact)
    place = (lax.broadcasted_iota(jnp.int32, (TEXT, L_DEV), 0) == compact).astype(BF)
    hidden = gated(gate_ref, up_ref, pl.ds(*at), x_ref)
    out_ref[...] = jnp.dot(hidden, place, preferred_element_type=F32).astype(BF)


def text_tile(at, info, gate, up, x):
    return pl.pallas_call(
        functools.partial(text_tile_kernel, at),
        out_shape=jax.ShapeDtypeStruct((at[1], L_DEV), BF),
        in_specs=[smem()] + [vmem()] * 3,
        out_specs=vmem(),
        compiler_params=pltpu.CompilerParams(vmem_limit_bytes=24 * MIB),
        cost_estimate=pl.CostEstimate(
            flops=4 * TEXT * D * at[1], bytes_accessed=10_000_000, transcendentals=0
        ),
        name="text_tile",
    )(info, gate, up, x)


TILES = ((0, 256), (256, 256), (512, 176))


def speech_rows(info, gain_ref, pieces, xs, sem):
    copies = []
    for d in range(8):
        peer = lax.rem(info[0] + d, 8)
        for half in range(2):
            cols = pl.multiple_of((half * 8 + peer) * KPART, KPART)
            copies.append(
                pltpu.make_async_copy(
                    pieces[d].at[:, pl.ds(half * KPART, KPART)], xs.at[:, pl.ds(cols, KPART)], sem
                )
            )
    for copy in copies:
        copy.start()
    for copy in copies:
        copy.wait()
    normalize(gain_ref, ROWS, xs, xs)


def own_kernel(info, gain_ref, *refs):
    pieces, gate, up, out_ref, xs, sem = refs[:8], *refs[8:]
    speech_rows(info, gain_ref, pieces, xs, sem)
    for tile in TILES:
        at = pl.ds(*tile)
        out_ref[at, :] = gated(gate, up, at, xs)


def own_hidden(info, gain, pieces, gate, up):
    return pl.pallas_call(
        own_kernel,
        out_shape=jax.ShapeDtypeStruct((FPART, ROWS), BF),
        in_specs=[smem(), vmem()] + [anywhere()] * 8 + [vmem()] * 2,
        out_specs=vmem(),
        scratch_shapes=[pltpu.VMEM((ROWS, D), BF), pltpu.SemaphoreType.DMA],
        compiler_params=pltpu.CompilerParams(vmem_limit_bytes=24 * MIB),
        cost_estimate=pl.CostEstimate(
            flops=2 * ROWS * D * 2 * FPART, bytes_accessed=14_000_000, transcendentals=0
        ),
        name="own_hidden",
    )(info, gain, *pieces, gate, up)


def speech_kernel(info, gain_ref, *refs):
    pieces, gate, up, own_ref, texts = refs[:8], refs[8], refs[9], refs[10], refs[11:14]
    out_ref, xs, sem = refs[14:]
    s, dp = info[1], info[2]
    speech_rows(info, gain_ref, pieces, xs, sem)
    row = lax.broadcasted_iota(jnp.int32, (1, L_DEV), 1)
    sources = []
    for part in (s, 1 - s):
        source = jnp.full((1, L_DEV), -1, jnp.int32)
        for slot in range(2):
            u = dp * 4 + part * 2 + slot
            first = info[OFFSET_AT + u] - dp * L_DEV
            inside = (row >= first) & (row < first + info[ROWS_AT + u])
            source = jnp.where(inside, row - first + slot * MAXROWS, source)
        sources.append(source)
    slot_row = lax.broadcasted_iota(jnp.int32, (ROWS, L_DEV), 0)
    picks = [(slot_row == source).astype(BF) for source in sources]
    speech = (sources[0] >= 0) | (sources[1] >= 0)
    for (start, size), text_ref in zip(TILES, texts):
        at = pl.ds(start, size)
        placed = jnp.dot(own_ref[at, :], picks[0], preferred_element_type=F32) + jnp.dot(
            gated(gate, up, at, xs), picks[1], preferred_element_type=F32
        )
        out_ref[at, :] = jnp.where(speech, placed.astype(BF), text_ref[...])


def speech_hidden(info, gain, pieces, gate, up, own, texts):
    return pl.pallas_call(
        speech_kernel,
        out_shape=jax.ShapeDtypeStruct((FPART, L_DEV), BF),
        in_specs=[smem(), vmem()] + [anywhere()] * 8 + [vmem()] * 6,
        out_specs=vmem(),
        scratch_shapes=[pltpu.VMEM((ROWS, D), BF), pltpu.SemaphoreType.DMA],
        compiler_params=pltpu.CompilerParams(vmem_limit_bytes=24 * MIB),
        cost_estimate=pl.CostEstimate(
            flops=2 * ROWS * D * 2 * FPART, bytes_accessed=16_000_000, transcendentals=0
        ),
        name="speech_hidden",
    )(info, gain, *pieces, gate, up, own, *texts)


def per_device(
    mel_frames,
    utt_rows,
    utt_owner,
    utt_offset,
    conv1_w,
    conv2_w,
    adapter_w,
    text_rows,
    norm_gain,
    gate_w,
    up_w,
):
    s = lax.axis_index("section")
    place = [lax.axis_index("mp"), s, lax.axis_index("dp")]
    info = jnp.concatenate(
        [jnp.stack(place + [0] * 5).astype(jnp.int32), utt_rows, utt_owner, utt_offset]
    )
    def stage(values, *others):
        return lax.optimization_barrier((*values, *others))[: len(values)]

    def hop(forth, back):
        return shift_z(forth, 1), shift_z(back, 7)

    def last_hop(forth, back):
        half = forth.shape[0] // 2
        return jnp.concatenate(hop(forth[:half], back[half:]), 0)

    def by_offset(a, hops, last):
        return [a, hops[0][1], hops[1][1], hops[2][1], last, hops[2][0], hops[1][0], hops[0][0]]

    w1 = conv1_w.T
    w1_other = swap(w1)

    sent = pack(info, mel_frames.reshape(P_DEV, 4 * MELS))
    received = lax.all_to_all(sent, "dp", 0, 0, tiled=True)
    both = jnp.stack(stage((gate_w.T, up_w.T), sent))
    gathered = lax.all_gather(both, "dp", axis=0)
    load = load_rows(info, *stage((text_rows, w1, w1_other), sent, both))

    t1 = hop(load, load)
    w2, wa = stage((conv2_w.T, adapter_w), load)
    w2_other, wa_other = swap(w2), swap(wa)
    t2 = hop(*stage(t1, sent, w2_other, wa_other))
    load_other, *o1 = [swap(v) for v in stage((load, *t1), *t2)]
    t3 = hop(*t2)
    o2 = [swap(v) for v in stage(t2, load_other, *o1, *t3)]
    forth, back = stage(t3, received, *o1)
    t4 = step_z(jnp.where(s == 0, forth, back))
    received_other = swap(received)
    maps = encoder(
        info, received, received_other, *by_offset(load, (t1, t2, t3), t4), w2, w2_other
    )

    m1 = hop(*stage((maps, maps), *o2))
    o3 = [swap(v) for v in stage((*t3, t4), maps)]
    m2 = hop(*m1)
    gain = norm_gain.reshape(1, D)
    text = stage(by_offset(load, (t1, t2, t3), t4), *m1)
    normed = text_norm(info, gain, text, by_offset(load_other, (o1, o2, o3), o3[2]))
    m3 = hop(*stage(m2, normed))
    m4 = last_hop(*m3)
    speech = adapter(info, by_offset(maps, (m1, m2, m3), m4), adapter_w, wa_other)

    s1 = hop(speech, speech)
    (here,) = stage((gathered,), speech)
    weights = place_weights(here)
    o0 = swap(*stage((speech,), *weights))
    s2 = hop(*s1)
    o1 = [swap(v) for v in stage(s1, o0)]
    texts = [text_tile(TILES[0], info, *weights, stage((normed,), *s1)[0])]
    s3 = hop(*stage(s2, *o1, *texts))
    o2 = [swap(v) for v in stage(s2, *o1, *texts)]
    texts.append(text_tile(TILES[1], info, *weights, stage((normed,), *s2)[0]))
    s4 = last_hop(*stage(s3, *o2, *texts))
    o3 = [swap(v) for v in stage(s3, *o2, *texts)]
    texts.append(text_tile(TILES[2], info, *weights, stage((normed,), *s3)[0]))
    (end,) = stage((s4,), *o3, *texts)
    o4 = swap(end)
    own = own_hidden(info, gain, by_offset(speech, (s1, s2, s3), end), *weights)
    other = by_offset(o0, (o1, o2, o3), o4)
    return speech_hidden(info, gain, other, *weights, own, texts).T


def solution(mesh):
    cols = ("section", "mp")
    return jax.shard_map(
        per_device,
        mesh=mesh,
        in_specs=(
            P("dp", None),
            P(),
            P(),
            P(),
            P(None, cols),
            P(None, cols),
            P(None, cols),
            P("dp", cols),
            P(),
            P("dp", cols),
            P("dp", cols),
        ),
        out_specs=P("dp", cols),
        check_vma=False,
    )
```
